128 devices in a mesh: grp: 2 (over core), elem: 64 (over x, y, z).
Axes of the slice: x: 4, y: 4, z: 4, core: 2. Of those that a mesh axis runs over, the one named last changes fastest.
Arguments:
- state: float32 [2, 4, 512, 16384], P('grp', None, None, 'elem'), may hold values from -4 to 4
- mean_flow: float32 [3, 512, 16384], P(None, None, 'elem'), may hold values from -3 to 3
- jacobian: float32 [2, 512, 16384], P('grp', None, 'elem'), may hold values from 0.5 to 2
- send_elem: int32 [64, 64, 4], P('elem'), may hold values from 0 to 255
- recv_elem: int32 [64, 64, 4], P('elem'), may hold values from 0 to 255
- recv_count: int32 [64, 64], P('elem'), may hold values from 0 to 4, as said below
Outputs:
- state_out: float32 [2, 4, 512, 16384], P('grp', None, None, 'elem')
The draws below stay inside these ranges and needn't reach their ends.
Inputs may be any that keep to these rules, and one draw needn't show every extreme that they name: `recv_count`: live slots per pair; in every draw some acoustic device has all 4 slots live from every LES device.
All inputs are finite; a program needn't handle non-finite values.
Results may differ from the reference program's by a relative error of at most 0.0003.
Values sent between devices are 32-bit elements; how exact they have to be, the bound alone decides.
No kernel may reach another device: no remote copies, remote signals or barrier semaphores. Data moves between devices by JAX's collectives and lax.ppermute only.
A program may use at most 128 MiB of HBM per device.

```python
import math
import jax
import jax.numpy as jnp
import numpy as np
from jax import lax

NP = 8
NA = 6
EX = 16
EY = 8
EZ_DEV = 2
CAP = 4
NE = 16384
PADA = 256
N_ELEM = 64


def draw_recv_count(key, part):
    key = jax.random.fold_in(key, 11)
    key_hot, key_cold, key_busy, key_full = jax.random.split(key, 4)
    is_hot = jax.random.randint(key_hot, (1, N_ELEM), 0, 4) == 0
    cold_vals = jax.random.randint(key_cold, (N_ELEM, N_ELEM), 0, CAP // 2 + 1)
    busy_vals = jax.random.randint(key_busy, (N_ELEM, N_ELEM), CAP // 2, CAP + 1)
    counts = jnp.where(is_hot, busy_vals, cold_vals)
    full_row = jax.random.randint(key_full, (), 0, N_ELEM)
    counts = jnp.where(jnp.arange(N_ELEM)[:, None] == full_row, CAP, counts)
    return counts.astype(jnp.int32)


def node_signs():
    node_id = jnp.arange(NP ** 3, dtype=jnp.int32)
    parity = (node_id // (NP * NP) + node_id // NP % NP + node_id % NP) % 2
    return (1 - 2 * parity).astype(jnp.float32)


def rough_field(key, dims_shape, floor_amp, top_amp, exponent):
    key_amp, key_sign = jax.random.split(key)
    spread_amp = jax.random.uniform(key_amp, dims_shape, jnp.float32)
    spread_amp = floor_amp + (top_amp - floor_amp) * spread_amp ** exponent
    sign_shape = dims_shape[:-2] + (1, dims_shape[-1])
    elem_sign = (1 - 2 * jax.random.randint(key_sign, sign_shape, 0, 2)).astype(jnp.float32)
    return spread_amp * elem_sign * node_signs()[:, None]


def draw_state(key, part):
    key = jax.random.fold_in(key, 5)
    exponent = 1.0
    return rough_field(key, (2, 4, NP ** 3, NE), 2.5, 4.0, exponent)


def draw_mean_flow(key, part):
    key = jax.random.fold_in(key, 7)
    exponent = 1.0
    return rough_field(key, (3, NP ** 3, NE), 2.0, 3.0, exponent)


def plant(drawn, own_key, smallest, top_value):
    longest = drawn.shape.index(max(drawn.shape))
    spots = []
    for shift in (0, 1):
        where = [jax.random.randint(jax.random.fold_in(own_key, axis), (), 0, length) for axis, length in enumerate(drawn.shape)]
        where[longest] = (where[longest] + shift) % drawn.shape[longest]
        spots.append(tuple(where))
    return drawn.at[spots[0]].set(smallest).at[spots[1]].set(top_value)


def level_of(own_key, extent, shards, smallest, largest):
    factor_of = 1.0
    for position, shards_of in shards:
        draws = jax.random.uniform(jax.random.fold_in(jax.random.fold_in(own_key, 6), position), (shards_of,), jnp.float32, smallest / len(shards), largest / len(shards))
        factor_of = factor_of * jnp.repeat(jnp.exp(draws), extent[position] // shards_of).reshape((-1,) + (1,) * (len(extent) - 1 - position))
    return factor_of


def setup_inputs(seed: int = 0) -> dict:
    seeds = jax.random.split(jax.random.key(seed), 7)
    state = draw_state(jax.random.fold_in(seeds[6], 71), 0)
    mean_flow = draw_mean_flow(jax.random.fold_in(seeds[6], 71), 0)
    jacobian = jnp.clip(jnp.exp(math.log(2.0) - 1.3862944 * jax.random.uniform(seeds[2], (2, NP**3, NE), jnp.float32) ** level_of(seeds[2], (2, NP**3, NE), ((0, 2), (2, 64)), -0.2, 0.2)), 0.5, 2.0)
    send_elem = plant(jax.random.randint(seeds[3], (N_ELEM, N_ELEM, CAP), 0, EX * EY * EZ_DEV), jax.random.fold_in(seeds[3], 1), 0, (EX * EY * EZ_DEV) - 1).astype(jnp.int32)
    recv_elem = plant(jax.random.randint(seeds[4], (N_ELEM, N_ELEM, CAP), 0, EX * EY * EZ_DEV), jax.random.fold_in(seeds[4], 1), 0, (EX * EY * EZ_DEV) - 1).astype(jnp.int32)
    recv_count = draw_recv_count(jax.random.fold_in(seeds[6], 71), 0)
    return {"state": state, "mean_flow": mean_flow, "jacobian": jacobian, "send_elem": send_elem, "recv_elem": recv_elem, "recv_count": recv_count}


les_speed_sq = 9.0
ape_speed_sq = 4.0
time_step = 0.004
highest = lax.Precision.HIGHEST


def legendre_pair(points, node_pos):
    degree = points - 1
    before = np.ones(node_pos.shape[0])
    current = node_pos.copy()
    for order in range(2, degree + 1):
        after = ((2 * order - 1) * node_pos * current - (order - 1) * before) / order
        before = current
        current = after
    return current, before


def lobatto_tables(points):
    degree = points - 1
    node_pos = -np.cos(np.pi * np.arange(points) / degree)
    for sweep in range(100):
        top_vals, prev_vals = legendre_pair(points, node_pos)
        node_pos = node_pos - (node_pos * top_vals - prev_vals) / (points * top_vals)
    node_pos[0] = -1.0
    node_pos[points - 1] = 1.0
    node_vals, unused_vals = legendre_pair(points, node_pos)
    weights = 2.0 / (points * (points - 1) * node_vals ** 2)
    derivative = np.zeros((points, points))
    for target in range(points):
        for source in range(points):
            if target != source:
                derivative[target, source] = node_vals[target] / (node_vals[source] * (node_pos[target] - node_pos[source]))
    derivative[0, 0] = -points * (points - 1) / 4.0
    derivative[points - 1, points - 1] = points * (points - 1) / 4.0
    return node_pos, weights, derivative


def tensor_cube(vector):
    return np.kron(vector, np.kron(vector, vector))


def group_tables():
    les_pos, les_wts, les_deriv = lobatto_tables(NP)
    ape_pos, ape_wts, ape_deriv = lobatto_tables(NA)
    deriv_pad = np.zeros((NP, NP))
    deriv_pad[:NA, :NA] = ape_deriv
    wts_pad = np.ones(NP)
    wts_pad[:NA] = ape_wts
    inside = np.zeros(NP)
    inside[:NA] = 1.0
    lagrange = np.ones((NA, NP))
    for target in range(NA):
        for source in range(NP):
            for pivot_id in range(NP):
                if pivot_id != source:
                    lagrange[target, source] *= (ape_pos[target] - les_pos[pivot_id]) / (les_pos[source] - les_pos[pivot_id])
    compact = np.kron(lagrange, np.kron(lagrange, lagrange))
    place_table = np.zeros((NA ** 3, NP ** 3))
    for slot_id in range(NA ** 3):
        plane_k = slot_id // (NA * NA)
        plane_j = (slot_id // NA) % NA
        plane_i = slot_id % NA
        place_table[slot_id, (plane_k * NP + plane_j) * NP + plane_i] = 1.0
    interp = place_table.T @ compact
    compact_pad = np.zeros((PADA, NP ** 3))
    compact_pad[:NA ** 3] = compact
    place_pad = np.zeros((PADA, NP ** 3))
    place_pad[:NA ** 3] = place_table
    derivs = np.stack([les_deriv, deriv_pad])
    quadrature = np.stack([tensor_cube(les_wts), tensor_cube(wts_pad)])
    masks = np.stack([np.ones(NP ** 3), tensor_cube(inside)])
    return derivs, quadrature, masks, interp, compact_pad, place_pad


def gradients(fields, derivative):
    along_x = jnp.einsum('ai,vkjie->vkjae', derivative, fields, precision=highest)
    along_y = jnp.einsum('aj,vkjie->vkaie', derivative, fields, precision=highest)
    along_z = jnp.einsum('ak,vkjie->vajie', derivative, fields, precision=highest)
    return along_x, along_y, along_z


def lamb_vector(fields, grads):
    along_x, along_y, along_z = grads
    vort_x = along_y[2] - along_z[1]
    vort_y = along_z[0] - along_x[2]
    vort_z = along_x[1] - along_y[0]
    return jnp.stack([vort_y * fields[2] - vort_z * fields[1],
                      vort_z * fields[0] - vort_x * fields[2],
                      vort_x * fields[1] - vort_y * fields[0]])


def tendency(fields, grads, advect, speed_sq, source):
    along_x, along_y, along_z = grads
    carried = advect[0:1] * along_x + advect[1:2] * along_y + advect[2:3] * along_z
    momentum = source - carried[0:3] - jnp.stack([along_x[3], along_y[3], along_z[3]])
    pressure = -carried[3] - speed_sq * (along_x[0] + along_y[1] + along_z[2])
    return jnp.concatenate([momentum, pressure[None]], axis=0)


def plane_sum(fields, node_axis, stride, has_prev, has_next, upper_idx):
    lower_plane = lax.dynamic_slice_in_dim(fields, 0, 1, node_axis)
    upper_plane = lax.dynamic_slice_in_dim(fields, upper_idx, 1, node_axis)
    from_next = jnp.roll(lower_plane, -stride, axis=-1) * has_next
    from_prev = jnp.roll(upper_plane, stride, axis=-1) * has_prev
    fields = lax.dynamic_update_slice_in_dim(fields, lower_plane + from_prev, 0, node_axis)
    return lax.dynamic_update_slice_in_dim(fields, upper_plane + from_next, upper_idx, node_axis)


def summed_global(fields, upper_idx):
    elem_count = fields.shape[-1]
    element_id = jnp.arange(elem_count)
    east_pos = element_id % EX
    north_pos = (element_id // EX) % EY
    everywhere = jnp.ones(elem_count, jnp.float32)
    fields = plane_sum(fields, 3, 1, (east_pos > 0).astype(jnp.float32), (east_pos < EX - 1).astype(jnp.float32), upper_idx)
    fields = plane_sum(fields, 2, EX, (north_pos > 0).astype(jnp.float32), (north_pos < EY - 1).astype(jnp.float32), upper_idx)
    return plane_sum(fields, 1, EX * EY, everywhere, everywhere, upper_idx)


def advance_group(start, derivative, upper_idx, weight, speed_sq, source, flow_cube):
    weight_sum = summed_global(weight, upper_idx)

    def section_rate(fields):
        advect = fields[0:3] if flow_cube is None else flow_cube
        raw = tendency(fields, gradients(fields, derivative), advect, speed_sq, source)
        return summed_global(weight * raw, upper_idx) / weight_sum

    first = section_rate(start)
    second = section_rate(start + 0.5 * time_step * first)
    third = section_rate(start + 0.5 * time_step * second)
    fourth = section_rate(start + time_step * third)
    return start + (time_step / 6.0) * (first + 2.0 * second + 2.0 * third + fourth)


def reference(state, mean_flow, jacobian, send_elem, recv_elem, recv_count):
    derivs, quadrature, masks, interp, compact_pad, place_pad = group_tables()
    elem_total = state.shape[-1]
    elem_dev = elem_total // N_ELEM
    cube_shape = (NP, NP, NP, elem_total)
    les_start = state[0].reshape((4,) + cube_shape)
    ape_start = state[1].reshape((4,) + cube_shape)
    flow_cube = mean_flow.reshape((3,) + cube_shape)
    les_deriv = jnp.asarray(derivs[0], jnp.float32)
    ape_deriv = jnp.asarray(derivs[1], jnp.float32)
    les_weight = (jnp.asarray(quadrature[0], jnp.float32)[:, None] * jacobian[0]).reshape((1,) + cube_shape)
    ape_weight = (jnp.asarray(quadrature[1], jnp.float32)[:, None] * jacobian[1]).reshape((1,) + cube_shape)

    lamb = lamb_vector(les_start, gradients(les_start, les_deriv))
    lamb_flat = lamb.reshape(3 * NP ** 3, elem_total)
    slot_src = (jnp.arange(N_ELEM, dtype=jnp.int32)[:, None, None] * elem_dev + send_elem).reshape(-1)
    blocks = jnp.take(lamb_flat, slot_src, axis=1).T.reshape(-1, NP ** 3)
    blocks = jnp.dot(blocks, jnp.asarray(interp, jnp.float32).T, precision=highest).reshape(-1, 3 * NP ** 3)
    live = jnp.arange(CAP, dtype=jnp.int32)[None, None, :] < recv_count.T[:, :, None]
    target = jnp.arange(N_ELEM, dtype=jnp.int32)[None, :, None] * elem_dev + jnp.transpose(recv_elem, (1, 0, 2))
    target = jnp.where(live, target, elem_total).reshape(-1)
    source = jax.ops.segment_sum(blocks, target, num_segments=elem_total + 1)[:elem_total]
    source = source.T.reshape((3,) + cube_shape)

    zero_source = jnp.zeros((3,) + cube_shape, jnp.float32)
    les_end = advance_group(les_start, les_deriv, NP - 1, les_weight, les_speed_sq, zero_source, None)
    ape_end = advance_group(ape_start, ape_deriv, NA - 1, ape_weight, ape_speed_sq, source, flow_cube)
    ape_end = ape_end * jnp.asarray(masks[1], jnp.float32).reshape(1, NP, NP, NP, 1)
    return jnp.stack([les_end.reshape(4, NP ** 3, elem_total), ape_end.reshape(4, NP ** 3, elem_total)])
```

```python
import jax
import jax.numpy as jnp
import numpy as np
from jax import lax
from jax.experimental import pallas as pl
from jax.experimental.pallas import tpu as pltpu
from jax.sharding import PartitionSpec as P

NP = 8
NA = 6
EX = 16
EY = 8
LAYER = EX * EY
NODES = NP**3
PLANE = NP * NP
FIELDS = 4
COMP = NA**3
EDGE = 40
BLOCK = 1024
TILES = BLOCK // LAYER
EDGE_LO = 768
EDGE_HI = 896

les_speed_sq = 9.0
ape_speed_sq = 4.0
time_step = 0.004
f32 = jnp.float32
bf16 = jnp.bfloat16


def legendre_pair(points, node_pos):
    degree = points - 1
    before = np.ones(node_pos.shape[0])
    current = node_pos.copy()
    for order in range(2, degree + 1):
        after = ((2 * order - 1) * node_pos * current - (order - 1) * before) / order
        before = current
        current = after
    return (current, before)


def lobatto_tables(points):
    degree = points - 1
    node_pos = -np.cos(np.pi * np.arange(points) / degree)
    for sweep in range(100):
        top_vals, prev_vals = legendre_pair(points, node_pos)
        node_pos = node_pos - (node_pos * top_vals - prev_vals) / (points * top_vals)
    node_pos[0] = -1.0
    node_pos[points - 1] = 1.0
    node_vals, unused_vals = legendre_pair(points, node_pos)
    weights = 2.0 / (points * (points - 1) * node_vals**2)
    derivative = np.zeros((points, points))
    for target in range(points):
        for source in range(points):
            if target != source:
                derivative[target, source] = node_vals[target] / (
                    node_vals[source] * (node_pos[target] - node_pos[source])
                )
    derivative[0, 0] = -points * (points - 1) / 4.0
    derivative[points - 1, points - 1] = points * (points - 1) / 4.0
    return (node_pos, weights, derivative)


def split_np(table):
    high = table.astype(np.float32).astype(jnp.bfloat16)
    low = (table - high.astype(np.float64)).astype(np.float32).astype(jnp.bfloat16)
    return high, low


def tables():
    les_pos, les_wts, les_deriv = lobatto_tables(NP)
    ape_pos, ape_wts, ape_deriv = lobatto_tables(NA)
    deriv_pad = np.zeros((NP, NP))
    deriv_pad[:NA, :NA] = ape_deriv
    wts_pad = np.ones(NP)
    wts_pad[:NA] = ape_wts
    inside = np.zeros(NP)
    inside[:NA] = 1.0
    derivs = [les_deriv, deriv_pad]
    wts = [les_wts, wts_pad]
    masks = [np.ones(NP), inside]
    speeds = [les_speed_sq, ape_speed_sq]
    mats = []
    scalars = np.zeros((2, 128), np.float32)
    wtile = np.zeros((2, 2, NP, LAYER), np.float32)
    for g in range(2):
        both = np.concatenate(
            [np.kron(np.eye(NP), derivs[g]), np.kron(derivs[g], np.eye(NP))], axis=0
        )
        high, low = split_np(both)
        mats.append(np.concatenate([high, high, low], axis=1))
        scalars[g, :64] = derivs[g].reshape(-1)
        scalars[g, 64:72] = wts[g]
        scalars[g, 72:80] = masks[g]
        scalars[g, 80] = speeds[g]
        wtile[g, 0] = wts[g][:, None]
        wtile[g, 1] = masks[g][:, None]
    lagrange = np.ones((NA, NP))
    for target in range(NA):
        for source in range(NP):
            for pivot_id in range(NP):
                if pivot_id != source:
                    lagrange[target, source] *= (ape_pos[target] - les_pos[pivot_id]) / (
                        les_pos[source] - les_pos[pivot_id]
                    )
    compact = np.kron(lagrange, np.kron(lagrange, lagrange))
    interp = np.zeros((COMP + 2 * EDGE, NODES))
    interp[:COMP] = compact
    interp[COMP : COMP + NA * NA] = compact[: NA * NA]
    interp[COMP + EDGE : COMP + EDGE + NA * NA] = compact[COMP - NA * NA :]
    high, low = split_np(interp)
    interp_mats = np.stack([high, low])
    place = np.zeros((NA * PLANE, COMP))
    for slot in range(COMP):
        k, j, i = slot // (NA * NA), slot // NA % NA, slot % NA
        place[(k * NP + j) * NP + i, slot] = 1.0
    place_edge = np.zeros((PLANE, EDGE))
    place_edge[:, : NA * NA] = place[:PLANE, : NA * NA]
    return dict(
        mats=np.stack(mats),
        scalars=scalars,
        wtile=wtile,
        interp=interp_mats,
        place=np.concatenate([place, place], axis=1).astype(jnp.bfloat16),
        place_edge=np.concatenate([place_edge, place_edge], axis=1).astype(jnp.bfloat16),
    )


def dot(a, b):
    return lax.dot_general(a, b, (((1,), (0,)), ((), ())), preferred_element_type=f32)


def dot_nt(a, b):
    return lax.dot_general(a, b, (((1,), (1,)), ((), ())), preferred_element_type=f32)


def split(x):
    high = x.astype(bf16)
    return high, (x - high.astype(f32)).astype(bf16)


def lane_masks():
    lane = lax.broadcasted_iota(jnp.int32, (1, LAYER), 1)
    east = lane % EX
    return (
        (east > 0).astype(f32),
        (east < EX - 1).astype(f32),
        (lane >= EX).astype(f32),
        (lane < LAYER - EX).astype(f32),
    )


def pair_sum(lo, hi, stride, has_prev, has_next):
    return (
        lo + pltpu.roll(hi, stride, 1) * has_prev,
        hi + pltpu.roll(lo, LAYER - stride, 1) * has_next,
    )


def rows(start, size=NP):
    return pl.ds(pl.multiple_of(start, 8), size)


def sum_in_plane(ref, blocks, up, masks):
    px, nx, py, ny = masks
    for group in range(0, blocks, NP):
        count = min(NP, blocks - group)
        lo_at = pl.ds(group * PLANE, count * NP, stride=NP)
        hi_at = pl.ds(group * PLANE + up, count * NP, stride=NP)
        lo, hi = pair_sum(ref[lo_at, :], ref[hi_at, :], 1, px, nx)
        ref[lo_at, :] = lo
        ref[hi_at, :] = hi
        for k in range(group, group + count):
            lo_rows = rows(k * PLANE)
            hi_rows = rows(k * PLANE + up * NP)
            lo, hi = pair_sum(ref[lo_rows, :], ref[hi_rows, :], EX, py, ny)
            ref[lo_rows, :] = lo
            ref[hi_rows, :] = hi


def sum_inner(ref, fields, up):
    for f in range(fields):
        hi_rows = rows(f * NODES + up * PLANE, PLANE)
        lo_rows = rows((fields + f) * NODES, PLANE)
        both = ref[hi_rows, :] + ref[lo_rows, :]
        ref[hi_rows, :] = both
        ref[lo_rows, :] = both


def put_layers(ref, fields, row, value):
    ref[rows(row), :] = value[:, :LAYER]
    ref[rows(fields * NODES + row), :] = value[:, LAYER:]


def get_layers(ref, fields, at):
    low = ref[at, :]
    high = ref[slice(at.start + fields * NODES, at.stop + fields * NODES), :]
    return jnp.concatenate([low, high], axis=1)


def raw_stage(gid, up, scal, mats, v, w, flow, g, wr, lamb=None):
    is_les = gid == 0
    speed = scal[gid, 80]

    def body(k, carry):
        base = k * PLANE
        mat = mats[gid]
        for f in range(FIELDS):
            high, low = split(v[rows(f * NODES + base, PLANE), :])
            g[f] = dot(mat, jnp.concatenate([high, low, high], axis=0))
        d = [scal[gid, k * NP + q] for q in range(NP)]
        for j in range(NP):
            at = base + j * NP
            u = [v[rows(f * NODES + at), :] for f in range(FIELDS)]
            gx = [g[f, j * NP : (j + 1) * NP, :] for f in range(FIELDS)]
            gy = [g[f, PLANE + j * NP : PLANE + (j + 1) * NP, :] for f in range(FIELDS)]
            gz = []
            for f in range(FIELDS):
                total = d[0] * v[f * NODES + j * NP : f * NODES + (j + 1) * NP, :]
                for q in range(1, NP):
                    start = f * NODES + q * PLANE + j * NP
                    total = total + d[q] * v[start : start + NP, :]
                gz.append(total)
            a = [jnp.where(is_les, u[m], flow[rows(m * NODES + at), :]) for m in range(3)]
            carried = [a[0] * gx[f] + a[1] * gy[f] + a[2] * gz[f] for f in range(FIELDS)]
            weight = w[rows(at), :]
            press = (gx[3], gy[3], gz[3])
            for m in range(3):
                put_layers(wr, FIELDS, m * NODES + at, -weight * (carried[m] + press[m]))
            total = -weight * (carried[3] + speed * (gx[0] + gy[1] + gz[2]))
            put_layers(wr, FIELDS, 3 * NODES + at, total)
            if lamb is not None:
                vx = gy[2] - gz[1]
                vy = gz[0] - gx[2]
                vz = gx[1] - gy[0]
                lamb[rows(at), :] = vy * u[2] - vz * u[1]
                lamb[rows(NODES + at), :] = vz * u[0] - vx * u[2]
                lamb[rows(2 * NODES + at), :] = vx * u[1] - vy * u[0]
        return carry

    lax.fori_loop(0, NP, body, 0)


def put_planes(wr, up, up_out, down_out, fields):
    for f in range(fields):
        at = slice(f * PLANE, (f + 1) * PLANE)
        up_out[at, :] = wr[rows((fields + f) * NODES + up * PLANE, PLANE), :]
        down_out[at, :] = wr[f * NODES : f * NODES + PLANE, :]


def first_kernel(
    ids, scal, state, jac, flow, mats, wtile, interp, send, recv, count,
    block_out, wr_out, w_out, qw_out, up_out, down_out, g, lamb, comp,
):
    gid = ids[0]
    up = ids[1]
    masks = lane_masks()
    wi = wtile[gid, 0]
    wi = jnp.concatenate([wi, wi], axis=1)
    for k in range(NP):
        for j in range(NP):
            at = slice(k * PLANE + j * NP, k * PLANE + (j + 1) * NP)
            value = wi * (scal[gid, 64 + k] * scal[gid, 64 + j]) * jac[at, :]
            w_out[at, :] = value
            put_layers(qw_out, 1, k * PLANE + j * NP, value)
    raw_stage(gid, up, scal, mats, state, w_out, flow, g, wr_out, lamb)

    sum_in_plane(wr_out, 2 * FIELDS * NP, up, masks)
    put_planes(wr_out, up, up_out, down_out, FIELDS)
    sum_inner(wr_out, FIELDS, up)
    at = slice(FIELDS * PLANE, (FIELDS + 1) * PLANE)
    up_out[at, :] = w_out[rows(up * PLANE, PLANE), LAYER : 2 * LAYER]
    down_out[at, :] = w_out[0:PLANE, 0:LAYER]
    sum_in_plane(qw_out, 2 * NP, up, masks)
    sum_inner(qw_out, 1, up)
    peers = recv.shape[0]
    cap = recv.shape[1]
    slot = lax.broadcasted_iota(jnp.int32, (peers, cap), 1)
    target = jnp.where(slot < count[...], recv[...], -1).astype(f32)
    at = slice((FIELDS + 1) * PLANE, (FIELDS + 1) * PLANE + peers)
    up_out[at, :] = jnp.zeros((peers, LAYER), f32)
    down_out[at, :] = jnp.zeros((peers, LAYER), f32)
    up_out[at, 0:cap] = target
    down_out[at, 0:cap] = target

    @pl.when(gid == 0)
    def _():
        comp[3 * COMP : EDGE_LO, :] = jnp.zeros((EDGE_LO - 3 * COMP, 2 * LAYER), f32)
        comp[EDGE_LO + 3 * EDGE : EDGE_HI, :] = jnp.zeros((8, 2 * LAYER), f32)
        comp[EDGE_HI + 3 * EDGE : BLOCK, :] = jnp.zeros((8, 2 * LAYER), f32)
        for m in range(3):
            high, low = split(lamb[m * NODES : (m + 1) * NODES, :])
            got = dot(interp[0], high) + dot(interp[0], low) + dot(interp[1], high)
            comp[m * COMP : (m + 1) * COMP, :] = got[:COMP]
            comp[EDGE_LO + m * EDGE : EDGE_LO + (m + 1) * EDGE, :] = got[COMP : COMP + EDGE]
            comp[EDGE_HI + m * EDGE : EDGE_HI + (m + 1) * EDGE, :] = got[COMP + EDGE :]
        elem = lax.broadcasted_iota(jnp.int32, (peers, 2 * LAYER), 1)
        high, low = split(comp[...])
        for c in range(cap):
            pick = (send[:, c : c + 1] == elem).astype(f32).astype(bf16)
            got = dot_nt(pick, high) + dot_nt(pick, low)
            for t in range(TILES):
                value = got[:, t * LAYER : (t + 1) * LAYER]
                if t >= TILES - 2:
                    value = pltpu.roll(value, peers - 1 if t == TILES - 2 else 1, 0)
                block_out[pl.ds(t * cap + c, peers, stride=TILES * cap), :] = value


def add_planes(wr, up, from_below, from_above, fields):
    for f in range(fields):
        at = slice(f * PLANE, (f + 1) * PLANE)
        lo_rows = slice(f * NODES, f * NODES + PLANE)
        hi_rows = rows((fields + f) * NODES + up * PLANE, PLANE)
        wr[lo_rows, :] = wr[lo_rows, :] + from_below[at, :]
        wr[hi_rows, :] = wr[hi_rows, :] + from_above[at, :]


def pick_sum(blocks, target_cols, lanes):
    elem = lax.broadcasted_iota(jnp.int32, (target_cols[0].shape[0], 2 * LAYER), 1)
    pick = [(t == elem)[:, lanes].astype(f32).astype(bf16) for t in target_cols]
    high, low = split(jnp.transpose(blocks))
    pick = jnp.concatenate(pick, axis=0)
    return dot(high, pick) + dot(low, pick)


def second_kernel(
    ids, scal, block, recv, count, from_below, from_above, state, w, qw, flow, mats, place,
    place_edge, wr_in,
    wr_out, inv_out, acc_out, half_out, up_out, down_out, g, wr, v, src, edge,
):
    gid = ids[0]
    up = ids[1]
    masks = lane_masks()
    peers = recv.shape[0]
    cap = recv.shape[1]
    wr[...] = wr_in[...]
    inv_out[...] = qw[...]
    weights_at = slice(FIELDS * PLANE, (FIELDS + 1) * PLANE)
    edge[0:PLANE, :] = from_below[weights_at, :]
    edge[PLANE : 2 * PLANE, :] = from_above[weights_at, :]
    sum_in_plane(edge, 2, up, masks)
    add_planes(inv_out, up, edge.at[0:PLANE], edge.at[PLANE : 2 * PLANE], 1)
    inv_out[...] = 1.0 / inv_out[...]
    add_planes(wr, up, from_below, from_above, FIELDS)

    half_out[...] = state[...]

    @pl.when(gid == 1)
    def _():
        apeak = NA - 1
        slot = lax.broadcasted_iota(jnp.int32, (peers, cap), 1)
        target = jnp.where(slot < count[...], recv[...], -1)
        tiles = []
        for t in range(TILES):
            parts = [
                block[pl.ds(t * cap + c, peers, stride=TILES * cap), :] for c in range(cap)
            ]
            tiles.append(jnp.concatenate(parts, axis=0))
        cols = [target[:, c : c + 1] for c in range(cap)]
        own = pick_sum(jnp.concatenate(tiles[: TILES - 2], axis=1), cols, slice(0, 2 * LAYER))
        tables_at = slice((FIELDS + 1) * PLANE, (FIELDS + 1) * PLANE + peers)
        below = from_below[tables_at, :].astype(jnp.int32)
        above = from_above[tables_at, :].astype(jnp.int32)
        lo_edge = pick_sum(
            tiles[TILES - 2],
            [above[:, c : c + 1] for c in range(cap)],
            slice(0, LAYER),
        )
        hi_edge = pick_sum(
            tiles[TILES - 1],
            [below[:, c : c + 1] for c in range(cap)],
            slice(LAYER, 2 * LAYER),
        )
        for m in range(3):
            high, low = split(own[m * COMP : (m + 1) * COMP])
            full = dot(place[...], jnp.concatenate([high, low], axis=0))
            size = NA * PLANE
            full = full * w[0:size, :]
            for layer in range(2):
                start = (3 * layer + m) * NODES
                src[start : start + size, :] = full[:, layer * LAYER : (layer + 1) * LAYER]
                src[start + size : start + NODES, :] = jnp.zeros((NODES - size, LAYER), f32)
            high, low = split(hi_edge[m * EDGE : (m + 1) * EDGE])
            full = dot(place_edge[...], jnp.concatenate([high, low], axis=0))
            edge[m * PLANE : (m + 1) * PLANE, :] = full * from_below[weights_at, :]
            high, low = split(lo_edge[m * EDGE : (m + 1) * EDGE])
            full = dot(place_edge[...], jnp.concatenate([high, low], axis=0))
            edge[(3 + m) * PLANE : (4 + m) * PLANE, :] = full * from_above[weights_at, :]
        sum_in_plane(src, 6 * NP, apeak, masks)
        sum_in_plane(edge, 6, apeak, masks)
        sum_inner(src, 3, apeak)
        add_planes(src, apeak, edge.at[0 : 3 * PLANE], edge.at[3 * PLANE : 6 * PLANE], 3)
        for m in range(3):
            at = slice(m * NODES, (m + 1) * NODES)
            sigma = get_layers(src, 3, at) * get_layers(inv_out, 1, slice(0, NODES))
            half_out[at, :] = state[at, :] + (0.5 * time_step) * sigma

    for f in range(FIELDS):
        at = slice(f * NODES, (f + 1) * NODES)
        rate = get_layers(wr, FIELDS, at) * get_layers(inv_out, 1, slice(0, NODES))
        half = half_out[at, :]
        v[at, :] = half + (0.5 * time_step) * rate
        acc_out[at, :] = half + (half - state[at, :]) + (time_step / 6.0) * rate
    raw_stage(gid, up, scal, mats, v, w, flow, g, wr_out)
    sum_in_plane(wr_out, 2 * FIELDS * NP, up, masks)
    put_planes(wr_out, up, up_out, down_out, FIELDS)
    sum_inner(wr_out, FIELDS, up)


def later_kernel(step, share, ids, scal, from_below, from_above, state, half, w, inv, flow, mats, wr_in, acc_in,
                 wr_out, acc_out, up_out, down_out, g, wr, v):
    gid = ids[0]
    up = ids[1]
    masks = lane_masks()
    wr[...] = wr_in[...]
    add_planes(wr, up, from_below, from_above, FIELDS)
    for f in range(FIELDS):
        at = slice(f * NODES, (f + 1) * NODES)
        rate = get_layers(wr, FIELDS, at) * get_layers(inv, 1, slice(0, NODES))
        base = half[at, :]
        if step == time_step:
            base = base + (base - state[at, :])
        v[at, :] = base + step * rate
        acc_out[at, :] = acc_in[at, :] + share * rate
    raw_stage(gid, up, scal, mats, v, w, flow, g, wr_out)
    sum_in_plane(wr_out, 2 * FIELDS * NP, up, masks)
    put_planes(wr_out, up, up_out, down_out, FIELDS)
    sum_inner(wr_out, FIELDS, up)


def last_kernel(ids, scal, wtile, from_below, from_above, inv, wr_in, acc_in, out, wr):
    gid = ids[0]
    up = ids[1]
    wr[...] = wr_in[...]
    add_planes(wr, up, from_below, from_above, FIELDS)
    mi = wtile[gid, 1]
    mi = jnp.concatenate([mi, mi], axis=1)
    for k in range(NP):
        for j in range(NP):
            keep = mi * (scal[gid, 72 + k] * scal[gid, 72 + j])
            at = k * PLANE + j * NP
            scale = get_layers(inv, 1, slice(at, at + NP)) * (time_step / 6.0)
            for f in range(FIELDS):
                where = slice(f * NODES + at, f * NODES + at + NP)
                rate = scale * get_layers(wr, FIELDS, where)
                out[where, :] = keep * (acc_in[where, :] + rate)


SMEM = pl.BlockSpec(memory_space=pltpu.SMEM)
VMEM = pl.BlockSpec(memory_space=pltpu.VMEM)


def call(kernel, smem, args, outs, scratch):
    return pl.pallas_call(
        kernel,
        out_shape=[jax.ShapeDtypeStruct(s, f32) for s in outs],
        in_specs=[SMEM] * smem + [VMEM] * (len(args) - smem),
        out_specs=[VMEM] * len(outs),
        scratch_shapes=[pltpu.VMEM(s, f32) for s in scratch],
        compiler_params=pltpu.CompilerParams(vmem_limit_bytes=52 * 1024 * 1024),
    )(*args)


def on_device(state, mean_flow, jacobian, send_elem, recv_elem, recv_count):
    consts = tables()
    gid = lax.axis_index("grp").astype(jnp.int32)
    ids = jnp.stack([gid, jnp.where(gid == 0, NP - 1, NA - 1).astype(jnp.int32)])
    width = state.shape[-1]
    peers, cap = send_elem.shape[1:]
    state = state.reshape(FIELDS * NODES, width)
    flow = mean_flow.reshape(3 * NODES, width)
    jac = jacobian.reshape(NODES, width)
    send = send_elem.reshape(peers, cap)
    recv = recv_elem.reshape(peers, cap)
    count = recv_count.reshape(peers, 1)
    scal = jnp.asarray(consts["scalars"])
    mats = jnp.asarray(consts["mats"])
    wtile = jnp.asarray(consts["wtile"])
    interp = jnp.asarray(consts["interp"])
    place = jnp.asarray(consts["place"])
    place_edge = jnp.asarray(consts["place_edge"])
    full = (FIELDS * NODES, width)
    one = (NODES, width)
    layered = (2 * FIELDS * NODES, LAYER)
    one_layered = (2 * NODES, LAYER)
    thin = (FIELDS * PLANE, LAYER)
    grads = (FIELDS, 2 * PLANE, width)
    size = lax.axis_size("elem")
    up_pairs = [(i, (i + 1) % size) for i in range(size)]
    down_pairs = [(j, i) for i, j in up_pairs]

    def exchange(up_planes, down_planes):
        return (
            lax.ppermute(up_planes, "elem", up_pairs),
            lax.ppermute(down_planes, "elem", down_pairs),
        )

    thick = ((FIELDS + 1) * PLANE + peers, LAYER)
    block, wr, w, qw, up_planes, down_planes = call(
        first_kernel, 2,
        (ids, scal, state, jac, flow, mats, wtile, interp, send, recv, count),
        [(TILES * cap * peers, LAYER), layered, one, one_layered, thick, thick],
        [grads, (3 * NODES, width), (BLOCK, width)],
    )
    from_below, from_above = exchange(up_planes, down_planes)
    block = lax.all_to_all(block, "elem", split_axis=0, concat_axis=0, tiled=True)
    block = lax.ppermute(block, "grp", [(0, 1)])
    wr, inv, acc, half, up_planes, down_planes = call(
        second_kernel, 2,
        (ids, scal, block, recv, count, from_below, from_above, state, w, qw, flow, mats,
         place, place_edge, wr),
        [layered, one_layered, full, full, thin, thin],
        [grads, layered, full, (6 * NODES, LAYER), (6 * PLANE, LAYER)],
    )
    for step, share in ((0.5 * time_step, time_step / 3.0), (time_step, time_step / 3.0)):
        from_below, from_above = exchange(up_planes, down_planes)

        def kernel(*refs, step=step, share=share):
            later_kernel(step, share, *refs)

        wr, acc, up_planes, down_planes = call(
            kernel, 2,
            (ids, scal, from_below, from_above, state, half, w, inv, flow, mats, wr, acc),
            [layered, full, thin, thin],
            [grads, layered, full],
        )
    from_below, from_above = exchange(up_planes, down_planes)
    (out,) = call(
        last_kernel, 2,
        (ids, scal, wtile, from_below, from_above, inv, wr, acc),
        [full],
        [layered],
    )
    return out.reshape(1, FIELDS, NODES, width)


def solution(mesh):
    placed = (
        P("grp", None, None, "elem"),
        P(None, None, "elem"),
        P("grp", None, "elem"),
        P("elem", None, None),
        P("elem", None, None),
        P("elem", None),
    )
    return jax.shard_map(
        on_device,
        mesh=mesh,
        in_specs=placed,
        out_specs=P("grp", None, None, "elem"),
        check_vma=False,
    )
```

```python
import jax
import jax.numpy as jnp
import numpy as np
from jax import lax
from jax.experimental import pallas as pl
from jax.experimental.pallas import tpu as pltpu
from jax.sharding import PartitionSpec as P

NP = 8
NA = 6
EX = 16
EY = 8
LAYER = EX * EY
NODES = NP**3
PLANE = NP * NP
FIELDS = 4
COMP = NA**3
EDGE = 40
BLOCK = 1024
TILES = BLOCK // LAYER
EDGE_LO = 768
EDGE_HI = 896

les_speed_sq = 9.0
ape_speed_sq = 4.0
time_step = 0.004
f32 = jnp.float32
bf16 = jnp.bfloat16


def legendre_pair(points, node_pos):
    degree = points - 1
    before = np.ones(node_pos.shape[0])
    current = node_pos.copy()
    for order in range(2, degree + 1):
        after = ((2 * order - 1) * node_pos * current - (order - 1) * before) / order
        before = current
        current = after
    return (current, before)


def lobatto_tables(points):
    degree = points - 1
    node_pos = -np.cos(np.pi * np.arange(points) / degree)
    for sweep in range(100):
        top_vals, prev_vals = legendre_pair(points, node_pos)
        node_pos = node_pos - (node_pos * top_vals - prev_vals) / (points * top_vals)
    node_pos[0] = -1.0
    node_pos[points - 1] = 1.0
    node_vals, unused_vals = legendre_pair(points, node_pos)
    weights = 2.0 / (points * (points - 1) * node_vals**2)
    derivative = np.zeros((points, points))
    for target in range(points):
        for source in range(points):
            if target != source:
                derivative[target, source] = node_vals[target] / (
                    node_vals[source] * (node_pos[target] - node_pos[source])
                )
    derivative[0, 0] = -points * (points - 1) / 4.0
    derivative[points - 1, points - 1] = points * (points - 1) / 4.0
    return (node_pos, weights, derivative)


def split_np(table):
    high = table.astype(np.float32).astype(jnp.bfloat16)
    low = (table - high.astype(np.float64)).astype(np.float32).astype(jnp.bfloat16)
    return high, low


def tables():
    les_pos, les_wts, les_deriv = lobatto_tables(NP)
    ape_pos, ape_wts, ape_deriv = lobatto_tables(NA)
    mats = []
    for points, deriv in ((NP, les_deriv), (NA, ape_deriv)):
        wide = np.zeros((NP, NP))
        wide[:points, :points] = deriv
        both = np.concatenate(
            [np.kron(np.eye(points), wide), np.kron(deriv, np.eye(NP))], axis=0
        )
        high, low = split_np(both)
        mats.append(np.concatenate([high, high, low], axis=1))
    lagrange = np.ones((NA, NP))
    for target in range(NA):
        for source in range(NP):
            for pivot_id in range(NP):
                if pivot_id != source:
                    lagrange[target, source] *= (ape_pos[target] - les_pos[pivot_id]) / (
                        les_pos[source] - les_pos[pivot_id]
                    )
    compact = np.kron(lagrange, np.kron(lagrange, lagrange))
    interp = np.zeros((COMP + 2 * EDGE, NODES))
    interp[:COMP] = compact
    interp[COMP : COMP + NA * NA] = compact[: NA * NA]
    interp[COMP + EDGE : COMP + EDGE + NA * NA] = compact[COMP - NA * NA :]
    high, low = split_np(interp)
    place = np.zeros((NA * PLANE, COMP))
    for slot in range(COMP):
        k, j, i = slot // (NA * NA), slot // NA % NA, slot % NA
        place[(k * NP + j) * NP + i, slot] = 1.0
    place_edge = np.zeros((PLANE, EDGE))
    place_edge[:, : NA * NA] = place[:PLANE, : NA * NA]
    return dict(
        derivs=(les_deriv, ape_deriv),
        weights=(les_wts, ape_wts),
        mats=mats,
        interp=np.stack([high, low]),
        place=np.concatenate([place, place], axis=1).astype(jnp.bfloat16),
        place_edge=np.concatenate([place_edge, place_edge], axis=1).astype(jnp.bfloat16),
    )


CONSTS = tables()
POINTS = (NP, NA)
SPEEDS = (les_speed_sq, ape_speed_sq)


def dot(a, b):
    return lax.dot_general(a, b, (((1,), (0,)), ((), ())), preferred_element_type=f32)


def dot_nt(a, b):
    return lax.dot_general(a, b, (((1,), (1,)), ((), ())), preferred_element_type=f32)


def split(x):
    high = x.astype(bf16)
    return high, (x - high.astype(f32)).astype(bf16)


def lane_masks():
    lane = lax.broadcasted_iota(jnp.int32, (1, LAYER), 1)
    east = lane % EX
    return (
        (east > 0).astype(f32),
        (east < EX - 1).astype(f32),
        (lane >= EX).astype(f32),
        (lane < LAYER - EX).astype(f32),
    )


def pair_sum(lo, hi, stride, has_prev, has_next):
    return (
        lo + pltpu.roll(hi, stride, 1) * has_prev,
        hi + pltpu.roll(lo, LAYER - stride, 1) * has_next,
    )


def sum_in_plane(ref, blocks, up, masks):
    px, nx, py, ny = masks
    for group in range(0, blocks, NP):
        count = min(NP, blocks - group)
        lo_at = pl.ds(group * PLANE, count * NP, stride=NP)
        hi_at = pl.ds(group * PLANE + up, count * NP, stride=NP)
        lo, hi = pair_sum(ref[lo_at, :], ref[hi_at, :], 1, px, nx)
        ref[lo_at, :] = lo
        ref[hi_at, :] = hi
        for k in range(group, group + count):
            lo_rows = slice(k * PLANE, k * PLANE + NP)
            hi_rows = slice(k * PLANE + up * NP, k * PLANE + (up + 1) * NP)
            lo, hi = pair_sum(ref[lo_rows, :], ref[hi_rows, :], EX, py, ny)
            ref[lo_rows, :] = lo
            ref[hi_rows, :] = hi


def sum_inner(ref, fields, up):
    for f in range(fields):
        hi_rows = span(f * NODES + up * PLANE, PLANE)
        lo_rows = span((fields + f) * NODES, PLANE)
        both = ref[hi_rows, :] + ref[lo_rows, :]
        ref[hi_rows, :] = both
        ref[lo_rows, :] = both


def span(start, size=NP):
    return slice(start, start + size)


def put_layers(ref, fields, row, value):
    size = value.shape[0]
    ref[span(row, size), :] = value[:, :LAYER]
    ref[span(fields * NODES + row, size), :] = value[:, LAYER:]


def get_layers(ref, fields, row, size):
    return jnp.concatenate(
        [ref[span(row, size), :], ref[span(fields * NODES + row, size), :]], axis=1
    )


def z_derivative(d, k, points, v, f, j):
    total = None
    for q in range(points):
        if d[k, q] != 0.0:
            part = float(d[k, q]) * v[span(f * NODES + q * PLANE + j * NP), :]
            total = part if total is None else total + part
    return total


def raw_stage(group, mat, v, w, flow, g, wr, lamb=None):
    points = POINTS[group]
    d = CONSTS["derivs"][group]
    size = points * NP
    for k in range(points):
        base = k * PLANE
        for f in range(FIELDS):
            high, low = split(v[span(f * NODES + base, size), :])
            g[k % 2, f, : 2 * size, :] = dot(mat[...], jnp.concatenate([high, low, high], axis=0))
        for j in range(points):
            at = base + j * NP
            gx = [g[k % 2, f, span(j * NP), :] for f in range(FIELDS)]
            gy = [g[k % 2, f, span(size + j * NP), :] for f in range(FIELDS)]
            gz = [z_derivative(d, k, points, v, f, j) for f in range(FIELDS)]
            u = [v[span(m * NODES + at), :] for m in range(3)]
            a = u if group == 0 else [flow[span(m * NODES + at), :] for m in range(3)]
            carried = [a[0] * gx[f] + a[1] * gy[f] + a[2] * gz[f] for f in range(FIELDS)]
            weight = -w[span(at), :]
            press = (gx[3], gy[3], gz[3])
            for m in range(3):
                put_layers(wr, FIELDS, m * NODES + at, weight * (carried[m] + press[m]))
            total = weight * (carried[3] + SPEEDS[group] * (gx[0] + gy[1] + gz[2]))
            put_layers(wr, FIELDS, 3 * NODES + at, total)
            if lamb is not None:
                vx = gy[2] - gz[1]
                vy = gz[0] - gx[2]
                vz = gx[1] - gy[0]
                lamb[span(at), :] = vy * u[2] - vz * u[1]
                lamb[span(NODES + at), :] = vz * u[0] - vx * u[2]
                lamb[span(2 * NODES + at), :] = vx * u[1] - vy * u[0]


def put_planes(wr, up, up_out, down_out, fields):
    for f in range(fields):
        at = span(f * PLANE, PLANE)
        up_out[at, :] = wr[span((fields + f) * NODES + up * PLANE, PLANE), :]
        down_out[at, :] = wr[span(f * NODES, PLANE), :]


def finish_stage(group, mat, v, w, flow, g, wr, up_out, down_out, lamb=None):
    up = POINTS[group] - 1
    raw_stage(group, mat, v, w, flow, g, wr, lamb)
    sum_in_plane(wr, 2 * FIELDS * NP, up, lane_masks())
    put_planes(wr, up, up_out, down_out, FIELDS)
    sum_inner(wr, FIELDS, up)


def each_group(ids, body):
    for group in range(2):
        pl.when(ids[0] == group)(lambda group=group: body(group))


def columns(row_table):
    cap, peers = row_table.shape
    tile = jnp.concatenate([row_table, jnp.zeros((cap, LAYER - peers), f32)], axis=1)
    tile = jnp.concatenate([tile, jnp.zeros((NP - cap, LAYER), f32)], axis=0)
    return jnp.transpose(tile)[:peers, :]


def targets(recv, count):
    slot = lax.broadcasted_iota(jnp.int32, recv.shape, 0)
    return jnp.where(slot < count[...], recv[...], -1).astype(f32)


def first_kernel(
    ids, state, jac, flow, les_mat, ape_mat, recv, count,
    lamb_out, wr_out, w_out, qw_out, up_out, down_out, g,
):
    def body(group):
        up = POINTS[group] - 1
        points = POINTS[group]
        wts = np.ones(NP)
        wts[:points] = CONSTS["weights"][group]
        sub = lax.broadcasted_iota(jnp.int32, (NP, 2 * LAYER), 0)
        wi = jnp.zeros((NP, 2 * LAYER), f32)
        for i in range(NP):
            wi = jnp.where(sub == i, float(wts[i]), wi)
        for k in range(NP):
            for j in range(NP):
                at = k * PLANE + j * NP
                value = (wi * float(wts[k] * wts[j])) * jac[span(at), :]
                w_out[span(at), :] = value
                put_layers(qw_out, 1, at, value)
        finish_stage(
            group, (les_mat, ape_mat)[group], state, w_out, flow, g, wr_out, up_out, down_out,
            lamb_out if group == 0 else None,
        )
        at = span(FIELDS * PLANE, PLANE)
        up_out[at, :] = w_out[span(up * PLANE, PLANE), LAYER : 2 * LAYER]
        down_out[at, :] = w_out[0:PLANE, 0:LAYER]
        sum_in_plane(qw_out, 2 * NP, up, lane_masks())
        sum_inner(qw_out, 1, up)

    each_group(ids, body)
    cap, peers = recv.shape
    at = span((FIELDS + 1) * PLANE, NP)
    up_out[at, :] = jnp.zeros((NP, LAYER), f32)
    down_out[at, :] = jnp.zeros((NP, LAYER), f32)
    at = span((FIELDS + 1) * PLANE, cap)
    target = targets(recv, count)
    up_out[at, 0:peers] = target
    down_out[at, 0:peers] = target


def block_kernel(ids, lamb, interp, send, block_out, comp):
    cap, peers = send.shape

    @pl.when(ids[0] == 0)
    def _():
        comp[3 * COMP : EDGE_LO, :] = jnp.zeros((EDGE_LO - 3 * COMP, 2 * LAYER), f32)
        comp[EDGE_LO + 3 * EDGE : EDGE_HI, :] = jnp.zeros((8, 2 * LAYER), f32)
        comp[EDGE_HI + 3 * EDGE : BLOCK, :] = jnp.zeros((8, 2 * LAYER), f32)
        for m in range(3):
            high, low = split(lamb[m * NODES : (m + 1) * NODES, :])
            got = dot(interp[0], high) + dot(interp[0], low) + dot(interp[1], high)
            comp[m * COMP : (m + 1) * COMP, :] = got[:COMP]
            comp[EDGE_LO + m * EDGE : EDGE_LO + (m + 1) * EDGE, :] = got[COMP : COMP + EDGE]
            comp[EDGE_HI + m * EDGE : EDGE_HI + (m + 1) * EDGE, :] = got[COMP + EDGE :]
        elem = lax.broadcasted_iota(jnp.int32, (peers, 2 * LAYER), 1)
        high, low = split(comp[...])
        table = columns(send[...].astype(f32)).astype(jnp.int32)
        for c in range(cap):
            pick = (table[:, c : c + 1] == elem).astype(f32).astype(bf16)
            got = dot_nt(pick, high) + dot_nt(pick, low)
            for t in range(TILES):
                value = got[:, t * LAYER : (t + 1) * LAYER]
                if t >= TILES - 2:
                    value = pltpu.roll(value, peers - 1 if t == TILES - 2 else 1, 0)
                block_out[pl.ds(t * cap + c, peers, stride=TILES * cap), :] = value


def add_planes(wr, up, from_below, from_above, fields):
    for f in range(fields):
        at = span(f * PLANE, PLANE)
        lo_rows = span(f * NODES, PLANE)
        hi_rows = span((fields + f) * NODES + up * PLANE, PLANE)
        wr[lo_rows, :] = wr[lo_rows, :] + from_below[at, :]
        wr[hi_rows, :] = wr[hi_rows, :] + from_above[at, :]


def pick_sum(blocks, table, cap, lanes):
    elem = lax.broadcasted_iota(jnp.int32, (table.shape[0], 2 * LAYER), 1).astype(f32)
    pick = [(table[:, c : c + 1] == elem)[:, lanes].astype(f32).astype(bf16) for c in range(cap)]
    high, low = split(jnp.transpose(blocks))
    pick = jnp.concatenate(pick, axis=0)
    return dot(high, pick) + dot(low, pick)


def update(group, half, state, wr, inv, v, step, acc_in, acc_out, share):
    points = POINTS[group]
    size = points * NP
    for k in range(points):
        scale = get_layers(inv, 1, k * PLANE, size)
        for f in range(FIELDS):
            at = f * NODES + k * PLANE
            rate = get_layers(wr, FIELDS, at, size) * scale
            base = half[span(at, size), :]
            if state is not None:
                start = state[span(at, size), :]
            if step == time_step:
                base = base + (base - start)
            v[span(at, size), :] = base + step * rate
            if acc_in is None:
                before = base + (base - start)
            else:
                before = acc_in[span(at, size), :]
            acc_out[span(at, size), :] = before + share * rate


def second_kernel(
    ids, block, recv, count, from_below, from_above, state, w, qw, flow, les_mat, ape_mat, place,
    place_edge, wr_in,
    wr_out, inv_out, acc_out, half_out, up_out, down_out, g, wr, v, src, edge,
):
    cap, peers = recv.shape
    weights_at = span(FIELDS * PLANE, PLANE)

    def source():
        up = NA - 1
        masks = lane_masks()
        tiles = []
        for t in range(TILES):
            parts = [
                block[pl.ds(t * cap + c, peers, stride=TILES * cap), :] for c in range(cap)
            ]
            tiles.append(jnp.concatenate(parts, axis=0))
        tables_at = span((FIELDS + 1) * PLANE, cap)
        own = columns(targets(recv, count))
        below = columns(from_below[tables_at, 0:peers])
        above = columns(from_above[tables_at, 0:peers])
        own = pick_sum(
            jnp.concatenate(tiles[: TILES - 2], axis=1), own, cap, slice(0, 2 * LAYER)
        )
        lo_edge = pick_sum(tiles[TILES - 2], above, cap, slice(0, LAYER))
        hi_edge = pick_sum(tiles[TILES - 1], below, cap, slice(LAYER, 2 * LAYER))
        for m in range(3):
            high, low = split(own[m * COMP : (m + 1) * COMP])
            full = dot(place[...], jnp.concatenate([high, low], axis=0))
            size = NA * PLANE
            put_layers(src, 3, m * NODES, full * w[0:size, :])
            high, low = split(hi_edge[m * EDGE : (m + 1) * EDGE])
            full = dot(place_edge[...], jnp.concatenate([high, low], axis=0))
            edge[span(m * PLANE, PLANE), :] = full * from_below[weights_at, :]
            high, low = split(lo_edge[m * EDGE : (m + 1) * EDGE])
            full = dot(place_edge[...], jnp.concatenate([high, low], axis=0))
            edge[span((3 + m) * PLANE, PLANE), :] = full * from_above[weights_at, :]
        sum_in_plane(src, 6 * NP, up, masks)
        sum_in_plane(edge, 6, up, masks)
        sum_inner(src, 3, up)
        add_planes(src, up, edge.at[0 : 3 * PLANE], edge.at[3 * PLANE : 6 * PLANE], 3)
        size = NA * NP
        for k in range(NA):
            scale = (0.5 * time_step) * get_layers(inv_out, 1, k * PLANE, size)
            for f in range(FIELDS):
                at = f * NODES + k * PLANE
                value = state[span(at, size), :]
                if f < 3:
                    value = value + scale * get_layers(src, 3, at, size)
                half_out[span(at, size), :] = value

    def body(group):
        up = POINTS[group] - 1
        wr[...] = wr_in[...]
        inv_out[...] = qw[...]
        edge[0:PLANE, :] = from_below[weights_at, :]
        edge[PLANE : 2 * PLANE, :] = from_above[weights_at, :]
        sum_in_plane(edge, 2, up, lane_masks())
        add_planes(inv_out, up, edge.at[0:PLANE], edge.at[PLANE : 2 * PLANE], 1)
        inv_out[...] = 1.0 / inv_out[...]
        add_planes(wr, up, from_below, from_above, FIELDS)
        if group == 1:
            source()
        else:
            half_out[...] = state[...]
        update(group, half_out, state, wr, inv_out, v, 0.5 * time_step, None, acc_out,
               time_step / 6.0)
        finish_stage(
            group, (les_mat, ape_mat)[group], v, w, flow, g, wr_out, up_out, down_out
        )

    each_group(ids, body)


def later_kernel(
    step, ids, from_below, from_above, state, half, w, inv, flow, les_mat, ape_mat, wr_in, acc_in,
    wr_out, acc_out, up_out, down_out, g, wr, v,
):
    def body(group):
        wr[...] = wr_in[...]
        add_planes(wr, POINTS[group] - 1, from_below, from_above, FIELDS)
        update(group, half, state, wr, inv, v, step, acc_in, acc_out, time_step / 3.0)
        finish_stage(
            group, (les_mat, ape_mat)[group], v, w, flow, g, wr_out, up_out, down_out
        )

    each_group(ids, body)


def last_kernel(ids, from_below, from_above, inv, wr_in, acc_in, out, wr):
    def body(group):
        points = POINTS[group]
        size = points * NP
        wr[...] = wr_in[...]
        add_planes(wr, points - 1, from_below, from_above, FIELDS)
        keep = lax.broadcasted_iota(jnp.int32, (size, 2 * LAYER), 0) % NP < points
        for k in range(NP):
            for f in range(FIELDS):
                at = f * NODES + k * PLANE
                done = 0
                if k < points:
                    scale = get_layers(inv, 1, k * PLANE, size) * (time_step / 6.0)
                    rate = get_layers(wr, FIELDS, at, size) * scale
                    value = acc_in[span(at, size), :] + rate
                    if points < NP:
                        value = jnp.where(keep, value, 0.0)
                    out[span(at, size), :] = value
                    done = size
                if done < PLANE:
                    out[span(at + done, PLANE - done), :] = jnp.zeros(
                        (PLANE - done, 2 * LAYER), f32
                    )

    each_group(ids, body)


SMEM = pl.BlockSpec(memory_space=pltpu.SMEM)
VMEM = pl.BlockSpec(memory_space=pltpu.VMEM)


def call(kernel, args, outs, scratch, megabytes=24):
    return pl.pallas_call(
        kernel,
        out_shape=[jax.ShapeDtypeStruct(s, f32) for s in outs],
        in_specs=[SMEM] + [VMEM] * (len(args) - 1),
        out_specs=[VMEM] * len(outs),
        scratch_shapes=[pltpu.VMEM(s, f32) for s in scratch],
        compiler_params=pltpu.CompilerParams(vmem_limit_bytes=megabytes * 1024 * 1024),
    )(*args)


def on_device(state, mean_flow, jacobian, send_elem, recv_elem, recv_count):
    ids = lax.axis_index("grp").astype(jnp.int32).reshape(1)
    width = state.shape[-1]
    peers, cap = send_elem.shape[1:]
    state = state.reshape(FIELDS * NODES, width)
    flow = mean_flow.reshape(3 * NODES, width)
    jac = jacobian.reshape(NODES, width)
    send = jnp.swapaxes(send_elem, 1, 2).reshape(cap, peers)
    recv = jnp.swapaxes(recv_elem, 1, 2).reshape(cap, peers)
    les_mat, ape_mat = (jnp.asarray(m) for m in CONSTS["mats"])
    interp = jnp.asarray(CONSTS["interp"])
    place = jnp.asarray(CONSTS["place"])
    place_edge = jnp.asarray(CONSTS["place_edge"])
    full = (FIELDS * NODES, width)
    one = (NODES, width)
    layered = (2 * FIELDS * NODES, LAYER)
    one_layered = (2 * NODES, LAYER)
    thin = (FIELDS * PLANE, LAYER)
    thick = ((FIELDS + 1) * PLANE + NP, LAYER)
    grads = (2, FIELDS, 2 * PLANE, width)
    size = lax.axis_size("elem")
    up_pairs = [(i, (i + 1) % size) for i in range(size)]
    down_pairs = [(j, i) for i, j in up_pairs]

    def exchange(up_planes, down_planes):
        return (
            lax.ppermute(up_planes, "elem", up_pairs),
            lax.ppermute(down_planes, "elem", down_pairs),
        )

    lamb, wr, w, qw, up_planes, down_planes = call(
        first_kernel,
        (ids, state, jac, flow, les_mat, ape_mat, recv, recv_count),
        [(3 * NODES, width), layered, one, one_layered, thick, thick],
        [grads],
    )
    from_below, from_above = exchange(up_planes, down_planes)
    (block,) = call(
        block_kernel,
        (ids, lamb, interp, send),
        [(TILES * cap * peers, LAYER)],
        [(BLOCK, width)],
    )
    block = lax.all_to_all(block, "elem", split_axis=0, concat_axis=0, tiled=True)
    block = lax.ppermute(block, "grp", [(0, 1)])
    wr, inv, acc, half, up_planes, down_planes = call(
        second_kernel,
        (ids, block, recv, recv_count, from_below, from_above, state, w, qw, flow, les_mat,
         ape_mat, place, place_edge, wr),
        [layered, one_layered, full, full, thin, thin],
        [grads, layered, full, (6 * NODES, LAYER), (6 * PLANE, LAYER)],
    )
    for step in (0.5 * time_step, time_step):
        from_below, from_above = exchange(up_planes, down_planes)

        def kernel(*refs, step=step):
            later_kernel(step, *refs)

        wr, acc, up_planes, down_planes = call(
            kernel,
            (ids, from_below, from_above, state, half, w, inv, flow, les_mat, ape_mat, wr, acc),
            [layered, full, thin, thin],
            [grads, layered, full],
        )
    from_below, from_above = exchange(up_planes, down_planes)
    (out,) = call(
        last_kernel,
        (ids, from_below, from_above, inv, wr, acc),
        [full],
        [layered],
    )
    return out.reshape(1, FIELDS, NODES, width)


def solution(mesh):
    placed = (
        P("grp", None, None, "elem"),
        P(None, None, "elem"),
        P("grp", None, "elem"),
        P("elem", None, None),
        P("elem", None, None),
        P("elem", None),
    )
    return jax.shard_map(
        on_device,
        mesh=mesh,
        in_specs=placed,
        out_specs=P("grp", None, None, "elem"),
        check_vma=False,
    )
```

```python
import jax
import jax.numpy as jnp
import numpy as np
from jax import lax
from jax.experimental import pallas as pl
from jax.experimental.pallas import tpu as pltpu
from jax.sharding import PartitionSpec as P

NP = 8
NA = 6
EX = 16
EY = 8
LAYER = EX * EY
NODES = NP**3
PLANE = NP * NP
FIELDS = 4
COMP = NA**3
EDGE = 40
BLOCK = 1024
TILES = BLOCK // LAYER
EDGE_LO = 768
EDGE_HI = 896

les_speed_sq = 9.0
ape_speed_sq = 4.0
time_step = 0.004
f32 = jnp.float32
bf16 = jnp.bfloat16


def legendre_pair(points, node_pos):
    degree = points - 1
    before = np.ones(node_pos.shape[0])
    current = node_pos.copy()
    for order in range(2, degree + 1):
        after = ((2 * order - 1) * node_pos * current - (order - 1) * before) / order
        before = current
        current = after
    return (current, before)


def lobatto_tables(points):
    degree = points - 1
    node_pos = -np.cos(np.pi * np.arange(points) / degree)
    for sweep in range(100):
        top_vals, prev_vals = legendre_pair(points, node_pos)
        node_pos = node_pos - (node_pos * top_vals - prev_vals) / (points * top_vals)
    node_pos[0] = -1.0
    node_pos[points - 1] = 1.0
    node_vals, unused_vals = legendre_pair(points, node_pos)
    weights = 2.0 / (points * (points - 1) * node_vals**2)
    derivative = np.zeros((points, points))
    for target in range(points):
        for source in range(points):
            if target != source:
                derivative[target, source] = node_vals[target] / (
                    node_vals[source] * (node_pos[target] - node_pos[source])
                )
    derivative[0, 0] = -points * (points - 1) / 4.0
    derivative[points - 1, points - 1] = points * (points - 1) / 4.0
    return (node_pos, weights, derivative)


def split_np(table):
    high = table.astype(np.float32).astype(jnp.bfloat16)
    low = (table - high.astype(np.float64)).astype(np.float32).astype(jnp.bfloat16)
    return high, low


def tables():
    les_pos, les_wts, les_deriv = lobatto_tables(NP)
    ape_pos, ape_wts, ape_deriv = lobatto_tables(NA)
    mats = []
    for points, deriv in ((NP, les_deriv), (NA, ape_deriv)):
        wide = np.zeros((NP, NP))
        wide[:points, :points] = deriv
        both = np.concatenate(
            [np.kron(np.eye(points), wide), np.kron(deriv, np.eye(NP))], axis=0
        )
        high, low = split_np(both)
        mats.append(np.concatenate([high, high, low], axis=1))
    lagrange = np.ones((NA, NP))
    for target in range(NA):
        for source in range(NP):
            for pivot_id in range(NP):
                if pivot_id != source:
                    lagrange[target, source] *= (ape_pos[target] - les_pos[pivot_id]) / (
                        les_pos[source] - les_pos[pivot_id]
                    )
    compact = np.kron(lagrange, np.kron(lagrange, lagrange))
    interp = np.zeros((COMP + 2 * EDGE, NODES))
    interp[:COMP] = compact
    interp[COMP : COMP + NA * NA] = compact[: NA * NA]
    interp[COMP + EDGE : COMP + EDGE + NA * NA] = compact[COMP - NA * NA :]
    high, low = split_np(interp)
    place = np.zeros((NA * PLANE, COMP))
    for slot in range(COMP):
        k, j, i = slot // (NA * NA), slot // NA % NA, slot % NA
        place[(k * NP + j) * NP + i, slot] = 1.0
    place_edge = np.zeros((PLANE, EDGE))
    place_edge[:, : NA * NA] = place[:PLANE, : NA * NA]
    return dict(
        derivs=(les_deriv, ape_deriv),
        weights=(les_wts, ape_wts),
        mats=mats,
        interp=np.stack([high, low]),
        place=np.concatenate([place, place], axis=1).astype(jnp.bfloat16),
        place_edge=np.concatenate([place_edge, place_edge], axis=1).astype(jnp.bfloat16),
    )


CONSTS = tables()
POINTS = (NP, NA)
SPEEDS = (les_speed_sq, ape_speed_sq)


def dot(a, b):
    return lax.dot_general(a, b, (((1,), (0,)), ((), ())), preferred_element_type=f32)


def dot_nt(a, b):
    return lax.dot_general(a, b, (((1,), (1,)), ((), ())), preferred_element_type=f32)


def split(x):
    high = x.astype(bf16)
    return high, (x - high.astype(f32)).astype(bf16)


def lane_masks():
    lane = lax.broadcasted_iota(jnp.int32, (1, LAYER), 1)
    east = lane % EX
    return (
        (east > 0).astype(f32),
        (east < EX - 1).astype(f32),
        (lane >= EX).astype(f32),
        (lane < LAYER - EX).astype(f32),
    )


def pair_sum(lo, hi, stride, has_prev, has_next):
    return (
        lo + pltpu.roll(hi, stride, 1) * has_prev,
        hi + pltpu.roll(lo, LAYER - stride, 1) * has_next,
    )


def sum_in_plane(ref, blocks, up, masks):
    px, nx, py, ny = masks
    for group in range(0, blocks, NP):
        count = min(NP, blocks - group)
        lo_at = pl.ds(group * PLANE, count * NP, stride=NP)
        hi_at = pl.ds(group * PLANE + up, count * NP, stride=NP)
        lo, hi = pair_sum(ref[lo_at, :], ref[hi_at, :], 1, px, nx)
        ref[lo_at, :] = lo
        ref[hi_at, :] = hi
        for k in range(group, group + count):
            lo_rows = slice(k * PLANE, k * PLANE + NP)
            hi_rows = slice(k * PLANE + up * NP, k * PLANE + (up + 1) * NP)
            lo, hi = pair_sum(ref[lo_rows, :], ref[hi_rows, :], EX, py, ny)
            ref[lo_rows, :] = lo
            ref[hi_rows, :] = hi


def sum_inner(ref, fields, up):
    for f in range(fields):
        hi_rows = span(f * NODES + up * PLANE, PLANE)
        lo_rows = span((fields + f) * NODES, PLANE)
        both = ref[hi_rows, :] + ref[lo_rows, :]
        ref[hi_rows, :] = both
        ref[lo_rows, :] = both


def span(start, size=NP):
    return slice(start, start + size)


def put_layers(ref, fields, row, value):
    size = value.shape[0]
    ref[span(row, size), :] = value[:, :LAYER]
    ref[span(fields * NODES + row, size), :] = value[:, LAYER:]


def get_layers(ref, fields, row, size):
    return jnp.concatenate(
        [ref[span(row, size), :], ref[span(fields * NODES + row, size), :]], axis=1
    )


def z_derivative(d, k, planes, v, f, j, lanes=slice(None)):
    total = None
    for q in planes:
        if d[k, q] != 0.0:
            part = float(d[k, q]) * v[span(f * NODES + q * PLANE + j * NP), lanes]
            total = part if total is None else total + part
    return total


def raw_stage(group, mat, v, w, flow, g, wr):
    points = POINTS[group]
    d = CONSTS["derivs"][group]
    size = points * NP
    for k in range(points):
        base = k * PLANE
        for f in range(FIELDS):
            high, low = split(v[span(f * NODES + base, size), :])
            g[k % 2, f, : 2 * size, :] = dot(mat[...], jnp.concatenate([high, low, high], axis=0))
        for j in range(points):
            at = base + j * NP
            gx = [g[k % 2, f, span(j * NP), :] for f in range(FIELDS)]
            gy = [g[k % 2, f, span(size + j * NP), :] for f in range(FIELDS)]
            gz = [z_derivative(d, k, range(points), v, f, j) for f in range(FIELDS)]
            u = [v[span(m * NODES + at), :] for m in range(3)]
            a = u if group == 0 else [flow[span(m * NODES + at), :] for m in range(3)]
            carried = [a[0] * gx[f] + a[1] * gy[f] + a[2] * gz[f] for f in range(FIELDS)]
            weight = -w[span(at), :]
            press = (gx[3], gy[3], gz[3])
            for m in range(3):
                put_layers(wr, FIELDS, m * NODES + at, weight * (carried[m] + press[m]))
            total = weight * (carried[3] + SPEEDS[group] * (gx[0] + gy[1] + gz[2]))
            put_layers(wr, FIELDS, 3 * NODES + at, total)


def edge_lanes(ref, row, up, size=NP):
    return jnp.concatenate(
        [ref[span(row, size), :LAYER], ref[span(row + up * PLANE, size), LAYER:]], axis=1
    )


def get_edges(ref, row, size=NP):
    return jnp.concatenate(
        [ref[span(row, size), :], ref[span(FIELDS * PLANE + row, size), :]], axis=1
    )


def put_edges(ref, row, value):
    size = value.shape[0]
    ref[span(row, size), :] = value[:, :LAYER]
    ref[span(FIELDS * PLANE + row, size), :] = value[:, LAYER:]


def edge_stage(group, mat, v, vb, w, flow, g, up_out, down_out):
    points = POINTS[group]
    up = points - 1
    d = CONSTS["derivs"][group]
    size = points * NP
    for f in range(FIELDS):
        high, low = split(get_edges(vb, f * PLANE, size))
        g[f, : 2 * size, :] = dot(mat[...], jnp.concatenate([high, low, high], axis=0))
    for j in range(points):
        u = [get_edges(vb, f * PLANE + j * NP) for f in range(FIELDS)]
        gx = [g[f, span(j * NP), :] for f in range(FIELDS)]
        gy = [g[f, span(size + j * NP), :] for f in range(FIELDS)]
        gz = []
        for f in range(FIELDS):
            low = z_derivative(d, 0, range(1, points), v, f, j, slice(0, LAYER))
            high = z_derivative(d, up, range(up), v, f, j, slice(LAYER, 2 * LAYER))
            low = low + float(d[0, 0]) * u[f][:, :LAYER]
            high = high + float(d[up, up]) * u[f][:, LAYER:]
            gz.append(jnp.concatenate([low, high], axis=1))
        a = u if group == 0 else [edge_lanes(flow, m * NODES + j * NP, up) for m in range(3)]
        weight = -edge_lanes(w, j * NP, up)
        carried = [a[0] * gx[f] + a[1] * gy[f] + a[2] * gz[f] for f in range(FIELDS)]
        press = (gx[3], gy[3], gz[3])
        values = [weight * (carried[m] + press[m]) for m in range(3)]
        values.append(weight * (carried[3] + SPEEDS[group] * (gx[0] + gy[1] + gz[2])))
        for f in range(FIELDS):
            down_out[span(f * PLANE + j * NP), :] = values[f][:, :LAYER]
            up_out[span(f * PLANE + j * NP), :] = values[f][:, LAYER:]
    masks = lane_masks()
    sum_in_plane(up_out, FIELDS, up, masks)
    sum_in_plane(down_out, FIELDS, up, masks)


def take_edges(group, ref, out):
    for f in range(FIELDS):
        put_edges(out, f * PLANE, edge_lanes(ref, f * NODES, POINTS[group] - 1, PLANE))


def inner_stage(group, mat, v, w, flow, g, wr):
    up = POINTS[group] - 1
    raw_stage(group, mat, v, w, flow, g, wr)
    sum_in_plane(wr, 2 * FIELDS * NP, up, lane_masks())
    sum_inner(wr, FIELDS, up)


def each_group(ids, body):
    for group in range(2):
        pl.when(ids[0] == group)(lambda group=group: body(group))


def columns(row_table):
    cap, peers = row_table.shape
    tile = jnp.concatenate([row_table, jnp.zeros((cap, LAYER - peers), f32)], axis=1)
    tile = jnp.concatenate([tile, jnp.zeros((NP - cap, LAYER), f32)], axis=0)
    return jnp.transpose(tile)[:peers, :]


def targets(recv, count):
    slot = lax.broadcasted_iota(jnp.int32, recv.shape, 0)
    return jnp.where(slot < count[...], recv[...], -1).astype(f32)


def weights(group, jac, planes):
    wts = np.ones(NP)
    wts[: POINTS[group]] = CONSTS["weights"][group]
    sub = lax.broadcasted_iota(jnp.int32, (NP, 2 * LAYER), 0)
    wi = jnp.zeros((NP, 2 * LAYER), f32)
    for i in range(NP):
        wi = jnp.where(sub == i, float(wts[i]), wi)
    for k in planes:
        for j in range(NP):
            at = k * PLANE + j * NP
            yield k, j, at, (wi * float(wts[k] * wts[j])) * jac[span(at), :]


def first_kernel(
    ids, state, jac, flow, les_mat, ape_mat,
    wr_out, w_out, qw_out, g,
):
    def body(group):
        up = POINTS[group] - 1
        for k, j, at, value in weights(group, jac, range(NP)):
            w_out[span(at), :] = value
            put_layers(qw_out, 1, at, value)
        inner_stage(group, (les_mat, ape_mat)[group], state, w_out, flow, g, wr_out)
        sum_in_plane(qw_out, 2 * NP, up, lane_masks())
        sum_inner(qw_out, 1, up)

    each_group(ids, body)


def edge_kernel(
    ids, state, jac_at, flow_at, les_at, ape_at, recv, count,
    up_out, down_out,
    v, jac, flow, les_mat, ape_mat, g, w, vb, sems,
):
    cap, peers = recv.shape
    sources = (state, jac_at, (les_at, ape_at), flow_at)
    places = (v, jac, (les_mat, ape_mat), flow)

    def body(group):
        copies = []
        for n in range(4 if group == 1 else 3):
            pick = (lambda x: x[group]) if n == 2 else (lambda x: x)
            copies.append(pltpu.make_async_copy(pick(sources[n]), pick(places[n]), sems.at[n]))
        for copy in copies:
            copy.start()
        at = span((FIELDS + 1) * PLANE, NP)
        up_out[at, :] = jnp.zeros((NP, LAYER), f32)
        down_out[at, :] = jnp.zeros((NP, LAYER), f32)
        at = span((FIELDS + 1) * PLANE, cap)
        target = targets(recv, count)
        up_out[at, 0:peers] = target
        down_out[at, 0:peers] = target
        for copy in copies:
            copy.wait()
        up = POINTS[group] - 1
        for k, j, at, value in weights(group, jac, (0, up)):
            w[span(at), :] = value
        take_edges(group, v, vb)
        edge_stage(group, (les_mat, ape_mat)[group], v, vb, w, flow, g, up_out, down_out)
        at = span(FIELDS * PLANE, PLANE)
        up_out[at, :] = w[span(up * PLANE, PLANE), LAYER:]
        down_out[at, :] = w[span(0, PLANE), :LAYER]

    each_group(ids, body)


def block_kernel(
    ids, state, les_at, interp_at, send_at,
    block_out,
    v, les_mat, interp, send, g, lamb, comp, sems,
):
    cap, peers = send.shape

    @pl.when(ids[0] == 0)
    def _():
        copies = [
            pltpu.make_async_copy(les_at, les_mat, sems.at[0]),
            pltpu.make_async_copy(state.at[0 : 3 * NODES, :], v, sems.at[1]),
            pltpu.make_async_copy(send_at, send, sems.at[2]),
            pltpu.make_async_copy(interp_at, interp, sems.at[3]),
        ]
        for copy in copies:
            copy.start()
        comp[3 * COMP : EDGE_LO, :] = jnp.zeros((EDGE_LO - 3 * COMP, 2 * LAYER), f32)
        comp[EDGE_LO + 3 * EDGE : EDGE_HI, :] = jnp.zeros((8, 2 * LAYER), f32)
        comp[EDGE_HI + 3 * EDGE : BLOCK, :] = jnp.zeros((8, 2 * LAYER), f32)
        copies[0].wait()
        copies[1].wait()
        d = CONSTS["derivs"][0]
        for k in range(NP):
            base = k * PLANE
            for f in range(3):
                high, low = split(v[span(f * NODES + base, PLANE), :])
                stack = jnp.concatenate([high, low, high], axis=0)
                some = (slice(PLANE, 2 * PLANE), slice(0, PLANE), slice(0, 2 * PLANE))[f]
                g[k % 2, f, some, :] = dot(les_mat[some, :], stack)
            for j in range(NP):
                at = base + j * NP
                gx = [None] + [g[k % 2, f, span(j * NP), :] for f in (1, 2)]
                gy = [g[k % 2, f, span(PLANE + j * NP), :] for f in (0, 2)]
                gz = [z_derivative(d, k, range(NP), v, f, j) for f in (0, 1)]
                u = [v[span(m * NODES + at), :] for m in range(3)]
                vx = gy[1] - gz[1]
                vy = gz[0] - gx[2]
                vz = gx[1] - gy[0]
                lamb[span(at), :] = vy * u[2] - vz * u[1]
                lamb[span(NODES + at), :] = vz * u[0] - vx * u[2]
                lamb[span(2 * NODES + at), :] = vx * u[1] - vy * u[0]
        copies[2].wait()
        copies[3].wait()
        for m in range(3):
            high, low = split(lamb[m * NODES : (m + 1) * NODES, :])
            got = dot(interp[0], high) + dot(interp[0], low) + dot(interp[1], high)
            comp[m * COMP : (m + 1) * COMP, :] = got[:COMP]
            comp[EDGE_LO + m * EDGE : EDGE_LO + (m + 1) * EDGE, :] = got[COMP : COMP + EDGE]
            comp[EDGE_HI + m * EDGE : EDGE_HI + (m + 1) * EDGE, :] = got[COMP + EDGE :]
        elem = lax.broadcasted_iota(jnp.int32, (peers, 2 * LAYER), 1)
        high, low = split(comp[...])
        table = columns(send[...].astype(f32)).astype(jnp.int32)
        pick = [(table[:, c : c + 1] == elem).astype(f32).astype(bf16) for c in range(cap)]
        pick = jnp.concatenate(pick, axis=0)
        got = dot_nt(pick, high) + dot_nt(pick, low)
        for c in range(cap):
            for t in range(TILES):
                value = got[span(c * peers, peers), t * LAYER : (t + 1) * LAYER]
                if t >= TILES - 2:
                    value = pltpu.roll(value, peers - 1 if t == TILES - 2 else 1, 0)
                block_out[pl.ds(t * cap + c, peers, stride=TILES * cap), :] = value


def add_planes(wr, up, from_below, from_above, fields):
    for f in range(fields):
        at = span(f * PLANE, PLANE)
        lo_rows = span(f * NODES, PLANE)
        hi_rows = span((fields + f) * NODES + up * PLANE, PLANE)
        wr[lo_rows, :] = wr[lo_rows, :] + from_below[at, :]
        wr[hi_rows, :] = wr[hi_rows, :] + from_above[at, :]


def pick_sum(blocks, table, cap, lanes):
    elem = lax.broadcasted_iota(jnp.int32, (table.shape[0], 2 * LAYER), 1).astype(f32)
    pick = [(table[:, c : c + 1] == elem)[:, lanes].astype(f32).astype(bf16) for c in range(cap)]
    high, low = split(jnp.transpose(blocks))
    pick = jnp.concatenate(pick, axis=0)
    return dot(high, pick) + dot(low, pick)


def summed(group, wr, f, k, size, from_below, from_above):
    at = f * NODES + k * PLANE
    low = wr[span(at, size), :]
    high = wr[span(FIELDS * NODES + at, size), :]
    if from_below is not None and k == 0:
        low = low + from_below[span(f * PLANE, size), :]
    if from_above is not None and k == POINTS[group] - 1:
        high = high + from_above[span(f * PLANE, size), :]
    return jnp.concatenate([low, high], axis=1)


def update(group, half, state, wr, inv, v, step, acc_in, acc_out, share, from_below, from_above):
    points = POINTS[group]
    size = points * NP
    for k in range(points):
        scale = get_layers(inv, 1, k * PLANE, size)
        for f in range(FIELDS):
            at = f * NODES + k * PLANE
            rate = summed(group, wr, f, k, size, from_below, from_above) * scale
            base = half[span(at, size), :]
            if acc_in is None or step == time_step:
                full = base + (base - state[span(at, size), :])
            if step == time_step:
                base = full
            v[span(at, size), :] = base + step * rate
            before = full if acc_in is None else acc_in[span(at, size), :]
            acc_out[span(at, size), :] = before + share * rate


def second_kernel(
    ids, block, recv, count, from_below, from_above, state, w, qw, flow, les_mat, ape_mat, place,
    place_edge, wr_in,
    v, inv_out, acc_out, half_out, acc_edges, up_out, down_out, g, vb, src, edge,
):
    cap, peers = recv.shape
    weights_at = span(FIELDS * PLANE, PLANE)

    def source():
        up = NA - 1
        masks = lane_masks()
        tiles = []
        for t in range(TILES):
            parts = [
                block[pl.ds(t * cap + c, peers, stride=TILES * cap), :] for c in range(cap)
            ]
            tiles.append(jnp.concatenate(parts, axis=0))
        tables_at = span((FIELDS + 1) * PLANE, cap)
        own = columns(targets(recv, count))
        below = columns(from_below[tables_at, 0:peers])
        above = columns(from_above[tables_at, 0:peers])
        own = pick_sum(
            jnp.concatenate(tiles[: TILES - 2], axis=1), own, cap, slice(0, 2 * LAYER)
        )
        lo_edge = pick_sum(tiles[TILES - 2], above, cap, slice(0, LAYER))
        hi_edge = pick_sum(tiles[TILES - 1], below, cap, slice(LAYER, 2 * LAYER))
        for m in range(3):
            high, low = split(own[m * COMP : (m + 1) * COMP])
            full = dot(place[...], jnp.concatenate([high, low], axis=0))
            size = NA * PLANE
            put_layers(src, 3, m * NODES, full * w[0:size, :])
            high, low = split(hi_edge[m * EDGE : (m + 1) * EDGE])
            full = dot(place_edge[...], jnp.concatenate([high, low], axis=0))
            edge[span(m * PLANE, PLANE), :] = full * from_below[weights_at, :]
            high, low = split(lo_edge[m * EDGE : (m + 1) * EDGE])
            full = dot(place_edge[...], jnp.concatenate([high, low], axis=0))
            edge[span((3 + m) * PLANE, PLANE), :] = full * from_above[weights_at, :]
        sum_in_plane(src, 6 * NP, up, masks)
        sum_in_plane(edge, 6, up, masks)
        sum_inner(src, 3, up)
        add_planes(src, up, edge.at[0 : 3 * PLANE], edge.at[3 * PLANE : 6 * PLANE], 3)
        size = NA * NP
        for k in range(NA):
            scale = (0.5 * time_step) * get_layers(inv_out, 1, k * PLANE, size)
            for f in range(FIELDS):
                at = f * NODES + k * PLANE
                value = state[span(at, size), :]
                if f < 3:
                    value = value + scale * get_layers(src, 3, at, size)
                half_out[span(at, size), :] = value

    def body(group):
        up = POINTS[group] - 1
        inv_out[...] = qw[...]
        edge[0:PLANE, :] = from_below[weights_at, :]
        edge[PLANE : 2 * PLANE, :] = from_above[weights_at, :]
        sum_in_plane(edge, 2, up, lane_masks())
        add_planes(inv_out, up, edge.at[0:PLANE], edge.at[PLANE : 2 * PLANE], 1)
        inv_out[...] = 1.0 / inv_out[...]
        if group == 1:
            source()
        else:
            half_out[...] = state[...]
        update(group, half_out, state, wr_in, inv_out, v, 0.5 * time_step, None, acc_out,
               time_step / 6.0, from_below, from_above)
        take_edges(group, v, vb)
        take_edges(group, acc_out, acc_edges)
        edge_stage(group, (les_mat, ape_mat)[group], v, vb, w, flow, g, up_out, down_out)

    each_group(ids, body)


def edge_rate(group, f, from_below, from_above, down, up_planes, inv):
    size = POINTS[group] * NP
    at = span(f * PLANE, size)
    low = down[at, :] + from_below[at, :]
    high = up_planes[at, :] + from_above[at, :]
    low = low * inv[span(0, size), :]
    high = high * inv[span(NODES + (POINTS[group] - 1) * PLANE, size), :]
    return jnp.concatenate([low, high], axis=1)


def edge_step_kernel(
    step, ids, from_below, from_above, down, up_planes, v, half, state, w, inv, flow, les_mat,
    ape_mat, acc_in,
    vb, acc_edges, up_out, down_out, g,
):
    def body(group):
        up = POINTS[group] - 1
        size = POINTS[group] * NP
        for f in range(FIELDS):
            rate = edge_rate(group, f, from_below, from_above, down, up_planes, inv)
            base = edge_lanes(half, f * NODES, up, size)
            if step == time_step:
                base = base + (base - edge_lanes(state, f * NODES, up, size))
            put_edges(vb, f * PLANE, base + step * rate)
            before = get_edges(acc_in, f * PLANE, size)
            put_edges(acc_edges, f * PLANE, before + (time_step / 3.0) * rate)
        edge_stage(group, (les_mat, ape_mat)[group], v, vb, w, flow, g, up_out, down_out)

    each_group(ids, body)


def inner_kernel(step, ids, v_in, *refs):
    if step == 0.5 * time_step:
        half, state, w, inv, flow, les_mat, ape_mat, acc_in, v_out, acc_out, g, wr = refs
        v = v_in
    else:
        vb, half, state, w, inv, flow, les_mat, ape_mat, acc_in = refs[:9]
        g, wr, v = refs[-3:]
        v_out, acc_out = (refs[9], refs[10]) if step is not None else (None, refs[9])

    def body(group):
        if v is not v_in:
            v[...] = v_in[...]
            for f in range(FIELDS):
                size = POINTS[group] * NP
                up = POINTS[group] - 1
                value = get_edges(vb, f * PLANE, size)
                v[span(f * NODES, size), :LAYER] = value[:, :LAYER]
                v[span(f * NODES + up * PLANE, size), LAYER:] = value[:, LAYER:]
        inner_stage(group, (les_mat, ape_mat)[group], v, w, flow, g, wr)
        if step is None:
            finish(group, wr, inv, acc_in, acc_out)
        else:
            update(group, half, state, wr, inv, v_out, step, acc_in, acc_out, time_step / 3.0,
                   None, None)

    each_group(ids, body)


def finish(group, wr, inv, acc_in, out):
    points = POINTS[group]
    size = points * NP
    keep = lax.broadcasted_iota(jnp.int32, (size, 2 * LAYER), 0) % NP < points
    for k in range(NP):
        for f in range(FIELDS):
            at = f * NODES + k * PLANE
            done = 0
            if k < points:
                scale = get_layers(inv, 1, k * PLANE, size) * (time_step / 6.0)
                rate = summed(group, wr, f, k, size, None, None) * scale
                value = acc_in[span(at, size), :] + rate
                if points < NP:
                    value = jnp.where(keep, value, 0.0)
                out[span(at, size), :] = value
                done = size
            if done < PLANE:
                out[span(at + done, PLANE - done), :] = jnp.zeros((PLANE - done, 2 * LAYER), f32)


def last_kernel(
    ids, from_below, from_above, down, up_planes, inv, acc_edges, inner, out, planes, sems
):
    def body(group):
        points = POINTS[group]
        size = points * NP
        keep = lax.broadcasted_iota(jnp.int32, (size, 2 * LAYER), 0) % NP < points
        copies = []
        for f in range(FIELDS):
            rate = edge_rate(group, f, from_below, from_above, down, up_planes, inv)
            value = get_edges(acc_edges, f * PLANE, size) + (time_step / 6.0) * rate
            if points < NP:
                value = jnp.where(keep, value, 0.0)
            put_edges(planes, f * PLANE, value)
            for side in range(2):
                row = f * NODES + side * (points - 1) * PLANE
                copies.append(
                    pltpu.make_async_copy(
                        planes.at[span((side * FIELDS + f) * PLANE, size), :],
                        out.at[span(row, size), side * LAYER : (side + 1) * LAYER],
                        sems.at[side * FIELDS + f],
                    )
                )
                copies[-1].start()
        for copy in copies:
            copy.wait()

    each_group(ids, body)


SMEM = pl.BlockSpec(memory_space=pltpu.SMEM)
VMEM = pl.BlockSpec(memory_space=pltpu.VMEM)


def call(kernel, args, outs, scratch, megabytes):
    return pl.pallas_call(
        kernel,
        out_shape=[jax.ShapeDtypeStruct(s, f32) for s in outs],
        in_specs=[SMEM] + [VMEM] * (len(args) - 1),
        out_specs=[VMEM] * len(outs),
        scratch_shapes=[pltpu.VMEM(s, f32) for s in scratch],
        compiler_params=pltpu.CompilerParams(vmem_limit_bytes=megabytes * 1024 * 1024),
    )(*args)


def on_device(state, mean_flow, jacobian, send_elem, recv_elem, recv_count):
    ids = lax.axis_index("grp").astype(jnp.int32).reshape(1)
    width = state.shape[-1]
    peers, cap = send_elem.shape[1:]
    state = state.reshape(FIELDS * NODES, width)
    flow = mean_flow.reshape(3 * NODES, width)
    jac = jacobian.reshape(NODES, width)
    send = jnp.swapaxes(send_elem, 1, 2).reshape(cap, peers)
    recv = jnp.swapaxes(recv_elem, 1, 2).reshape(cap, peers)
    les_mat, ape_mat = (jnp.asarray(m) for m in CONSTS["mats"])
    interp = jnp.asarray(CONSTS["interp"])
    place = jnp.asarray(CONSTS["place"])
    place_edge = jnp.asarray(CONSTS["place_edge"])
    full = (FIELDS * NODES, width)
    one = (NODES, width)
    layered = (2 * FIELDS * NODES, LAYER)
    one_layered = (2 * NODES, LAYER)
    thin = (FIELDS * PLANE, LAYER)
    edges = (2 * FIELDS * PLANE, LAYER)
    thick = ((FIELDS + 1) * PLANE + NP, LAYER)
    grads = (2, FIELDS, 2 * PLANE, width)
    size = lax.axis_size("elem")
    up_pairs = [(i, (i + 1) % size) for i in range(size)]
    down_pairs = [(j, i) for i, j in up_pairs]

    def exchange(up_planes, down_planes):
        return (
            lax.ppermute(up_planes, "elem", up_pairs),
            lax.ppermute(down_planes, "elem", down_pairs),
        )

    hbm = pl.BlockSpec(memory_space=pltpu.HBM)
    (block,) = pl.pallas_call(
        block_kernel,
        out_shape=[jax.ShapeDtypeStruct((TILES * cap * peers, LAYER), f32)],
        in_specs=[SMEM] + [hbm] * 4,
        out_specs=[VMEM],
        scratch_shapes=[
            pltpu.VMEM((3 * NODES, width), f32),
            pltpu.VMEM(les_mat.shape, bf16),
            pltpu.VMEM(interp.shape, bf16),
            pltpu.VMEM((cap, peers), jnp.int32),
            pltpu.VMEM(grads, f32),
            pltpu.VMEM((3 * NODES, width), f32),
            pltpu.VMEM((BLOCK, width), f32),
            pltpu.SemaphoreType.DMA((4,)),
        ],
        compiler_params=pltpu.CompilerParams(vmem_limit_bytes=62 * 1024 * 1024),
    )(ids, state, les_mat, interp, send)
    up_planes, down_planes = pl.pallas_call(
        edge_kernel,
        out_shape=[jax.ShapeDtypeStruct(thick, f32)] * 2,
        in_specs=[SMEM] + [hbm] * 5 + [VMEM] * 2,
        out_specs=[VMEM] * 2,
        scratch_shapes=[
            pltpu.VMEM(full, f32),
            pltpu.VMEM(one, f32),
            pltpu.VMEM((3 * NODES, width), f32),
            pltpu.VMEM(les_mat.shape, bf16),
            pltpu.VMEM(ape_mat.shape, bf16),
            pltpu.VMEM(grads[1:], f32),
            pltpu.VMEM(one, f32),
            pltpu.VMEM(edges, f32),
            pltpu.SemaphoreType.DMA((4,)),
        ],
        compiler_params=pltpu.CompilerParams(vmem_limit_bytes=62 * 1024 * 1024),
    )(ids, state, jac, flow, les_mat, ape_mat, recv, recv_count)
    from_below, from_above = exchange(up_planes, down_planes)
    block = lax.all_to_all(block, "elem", split_axis=0, concat_axis=0, tiled=True)
    block, from_below, from_above, late_state, late_jac, late_flow = lax.optimization_barrier(
        (block, from_below, from_above, state, jac, flow)
    )
    wr, w, qw = call(
        first_kernel,
        (ids, late_state, late_jac, late_flow, les_mat, ape_mat),
        [layered, one, one_layered],
        [grads],
        10,
    )
    block = lax.ppermute(block, "grp", [(0, 1)])
    v, inv, acc, half, acc_edges, up_planes, down_planes = call(
        second_kernel,
        (ids, block, recv, recv_count, from_below, from_above, state, w, qw, flow, les_mat,
         ape_mat, place, place_edge, wr),
        [full, one_layered, full, full, edges, thin, thin],
        [grads[1:], edges, (6 * NODES, LAYER), (6 * PLANE, LAYER)],
        20,
    )
    vb = None
    for step in (0.5 * time_step, time_step, None):
        from_below, from_above = exchange(up_planes, down_planes)

        def inner(*refs, step=step):
            inner_kernel(step, *refs)

        def edge_step(*refs, step=step):
            edge_step_kernel(step, *refs)

        rest = (half, state, w, inv, flow, les_mat, ape_mat, acc)
        if vb is None:
            v, acc = call(inner, (ids, v) + rest, [full, full], [grads, layered], 22)
        elif step is not None:
            v, acc = call(inner, (ids, v, vb) + rest, [full, full], [grads, layered, full], 22)
        else:
            (out,) = call(inner, (ids, v, vb) + rest, [full], [grads, layered, full], 22)
            break
        vb, acc_edges, up_planes, down_planes = call(
            edge_step,
            (ids, from_below, from_above, down_planes, up_planes, v, half, state, w, inv, flow,
             les_mat, ape_mat, acc_edges),
            [edges, edges, thin, thin],
            [grads[1:]],
            14,
        )
    out = pl.pallas_call(
        last_kernel,
        out_shape=jax.ShapeDtypeStruct(full, f32),
        in_specs=[SMEM] + [VMEM] * 6 + [hbm],
        out_specs=hbm,
        scratch_shapes=[pltpu.VMEM(edges, f32), pltpu.SemaphoreType.DMA((2 * FIELDS,))],
        input_output_aliases={7: 0},
        compiler_params=pltpu.CompilerParams(vmem_limit_bytes=6 * 1024 * 1024),
    )(ids, from_below, from_above, down_planes, up_planes, inv, acc_edges, out)
    return out.reshape(1, FIELDS, NODES, width)


def solution(mesh):
    placed = (
        P("grp", None, None, "elem"),
        P(None, None, "elem"),
        P("grp", None, "elem"),
        P("elem", None, None),
        P("elem", None, None),
        P("elem", None),
    )
    return jax.shard_map(
        on_device,
        mesh=mesh,
        in_specs=placed,
        out_specs=P("grp", None, None, "elem"),
        check_vma=False,
    )
```

```python
import jax
import jax.numpy as jnp
import numpy as np
from jax import lax
from jax.experimental import pallas as pl
from jax.experimental.pallas import tpu as pltpu
from jax.sharding import PartitionSpec as P

NP = 8
NA = 6
EX = 16
EY = 8
LAYER = EX * EY
NODES = NP**3
PLANE = NP * NP
FIELDS = 4
COMP = NA**3
EDGE = 40
BLOCK = 1024
TILES = BLOCK // LAYER
EDGE_LO = 768
EDGE_HI = 896

les_speed_sq = 9.0
ape_speed_sq = 4.0
time_step = 0.004
f32 = jnp.float32
bf16 = jnp.bfloat16


def legendre_pair(points, node_pos):
    degree = points - 1
    before = np.ones(node_pos.shape[0])
    current = node_pos.copy()
    for order in range(2, degree + 1):
        after = ((2 * order - 1) * node_pos * current - (order - 1) * before) / order
        before = current
        current = after
    return (current, before)


def lobatto_tables(points):
    degree = points - 1
    node_pos = -np.cos(np.pi * np.arange(points) / degree)
    for sweep in range(100):
        top_vals, prev_vals = legendre_pair(points, node_pos)
        node_pos = node_pos - (node_pos * top_vals - prev_vals) / (points * top_vals)
    node_pos[0] = -1.0
    node_pos[points - 1] = 1.0
    node_vals, unused_vals = legendre_pair(points, node_pos)
    weights = 2.0 / (points * (points - 1) * node_vals**2)
    derivative = np.zeros((points, points))
    for target in range(points):
        for source in range(points):
            if target != source:
                derivative[target, source] = node_vals[target] / (
                    node_vals[source] * (node_pos[target] - node_pos[source])
                )
    derivative[0, 0] = -points * (points - 1) / 4.0
    derivative[points - 1, points - 1] = points * (points - 1) / 4.0
    return (node_pos, weights, derivative)


def split_np(table):
    high = table.astype(np.float32).astype(jnp.bfloat16)
    low = (table - high.astype(np.float64)).astype(np.float32).astype(jnp.bfloat16)
    return high, low


def tables():
    les_pos, les_wts, les_deriv = lobatto_tables(NP)
    ape_pos, ape_wts, ape_deriv = lobatto_tables(NA)
    mats = []
    for points, deriv in ((NP, les_deriv), (NA, ape_deriv)):
        wide = np.zeros((NP, NP))
        wide[:points, :points] = deriv
        both = np.concatenate(
            [np.kron(np.eye(points), wide), np.kron(deriv, np.eye(NP))], axis=0
        )
        high, low = split_np(both)
        mats.append(np.concatenate([high, high, low], axis=1))
    lagrange = np.ones((NA, NP))
    for target in range(NA):
        for source in range(NP):
            for pivot_id in range(NP):
                if pivot_id != source:
                    lagrange[target, source] *= (ape_pos[target] - les_pos[pivot_id]) / (
                        les_pos[source] - les_pos[pivot_id]
                    )
    compact = np.kron(lagrange, np.kron(lagrange, lagrange))
    interp = np.zeros((COMP + 2 * EDGE, NODES))
    interp[:COMP] = compact
    interp[COMP : COMP + NA * NA] = compact[: NA * NA]
    interp[COMP + EDGE : COMP + EDGE + NA * NA] = compact[COMP - NA * NA :]
    high, low = split_np(interp)
    place = np.zeros((NA * PLANE, COMP))
    for slot in range(COMP):
        k, j, i = slot // (NA * NA), slot // NA % NA, slot % NA
        place[(k * NP + j) * NP + i, slot] = 1.0
    place_edge = np.zeros((PLANE, EDGE))
    place_edge[:, : NA * NA] = place[:PLANE, : NA * NA]
    return dict(
        derivs=(les_deriv, ape_deriv),
        weights=(les_wts, ape_wts),
        mats=mats,
        interp=np.stack([high, low]),
        place=np.concatenate([place, place], axis=1).astype(jnp.bfloat16),
        place_edge=np.concatenate([place_edge, place_edge], axis=1).astype(jnp.bfloat16),
    )


CONSTS = tables()
POINTS = (NP, NA)
SPEEDS = (les_speed_sq, ape_speed_sq)


def dot(a, b):
    return lax.dot_general(a, b, (((1,), (0,)), ((), ())), preferred_element_type=f32)


def dot_nt(a, b):
    return lax.dot_general(a, b, (((1,), (1,)), ((), ())), preferred_element_type=f32)


def split(x):
    high = x.astype(bf16)
    return high, (x - high.astype(f32)).astype(bf16)


def lane_masks():
    lane = lax.broadcasted_iota(jnp.int32, (1, LAYER), 1)
    east = lane % EX
    return (
        (east > 0).astype(f32),
        (east < EX - 1).astype(f32),
        (lane >= EX).astype(f32),
        (lane < LAYER - EX).astype(f32),
    )


def pair_sum(lo, hi, stride, has_prev, has_next):
    return (
        lo + pltpu.roll(hi, stride, 1) * has_prev,
        hi + pltpu.roll(lo, LAYER - stride, 1) * has_next,
    )


def sum_one_plane(ref, row, up, masks):
    px, nx, py, ny = masks
    lo_at = pl.ds(row, NP, stride=NP)
    hi_at = pl.ds(row + up, NP, stride=NP)
    lo, hi = pair_sum(ref[lo_at, :], ref[hi_at, :], 1, px, nx)
    ref[lo_at, :] = lo
    ref[hi_at, :] = hi
    lo_rows = span(row)
    hi_rows = span(row + up * NP)
    lo, hi = pair_sum(ref[lo_rows, :], ref[hi_rows, :], EX, py, ny)
    ref[lo_rows, :] = lo
    ref[hi_rows, :] = hi


def sum_in_plane(ref, blocks, up, masks):
    for block in range(blocks):
        sum_one_plane(ref, block * PLANE, up, masks)


def sum_inner(ref, fields, up):
    for f in range(fields):
        hi_rows = span(f * NODES + up * PLANE, PLANE)
        lo_rows = span((fields + f) * NODES, PLANE)
        both = ref[hi_rows, :] + ref[lo_rows, :]
        ref[hi_rows, :] = both
        ref[lo_rows, :] = both


def span(start, size=NP):
    return slice(start, start + size)


def put_layers(ref, fields, row, value):
    size = value.shape[0]
    ref[span(row, size), :] = value[:, :LAYER]
    ref[span(fields * NODES + row, size), :] = value[:, LAYER:]


def get_layers(ref, fields, row, size):
    return jnp.concatenate(
        [ref[span(row, size), :], ref[span(fields * NODES + row, size), :]], axis=1
    )


def z_derivative(d, k, planes, v, f, j, lanes=slice(None)):
    total = None
    for q in planes:
        if d[k, q] != 0.0:
            part = float(d[k, q]) * v[span(f * NODES + q * PLANE + j * NP), lanes]
            total = part if total is None else total + part
    return total


def z_derivatives(d, points, v, gz):
    for f in range(FIELDS):
        for j in range(points):
            at = [f * NODES + q * PLANE + j * NP for q in range(points)]
            u = [v[span(a), :] for a in at]
            half = points // 2
            even = [u[q] + u[points - 1 - q] for q in range(half)]
            odd = [u[q] - u[points - 1 - q] for q in range(half)]
            for k in range(half):
                first = second = None
                for q in range(half):
                    x = float(0.5 * (d[k, q] + d[k, points - 1 - q])) * even[q]
                    y = float(0.5 * (d[k, q] - d[k, points - 1 - q])) * odd[q]
                    first = x if first is None else first + x
                    second = y if second is None else second + y
                gz[span(at[k]), :] = second + first
                gz[span(at[points - 1 - k]), :] = second - first


def inner_stage(group, mat, v, w, flow, g, gz_at, wr, after=None):
    points = POINTS[group]
    up = points - 1
    d = CONSTS["derivs"][group]
    size = points * NP
    masks = lane_masks()
    z_derivatives(d, points, v, gz_at)
    for turn, k in enumerate([0, up] + list(range(1, up))):
        base = k * PLANE
        for f in range(FIELDS):
            high, low = split(v[span(f * NODES + base, size), :])
            g[turn % 2, f, : 2 * size, :] = dot(mat[...], jnp.concatenate([high, low, high], axis=0))
        for j in range(points):
            at = base + j * NP
            gx = [g[turn % 2, f, span(j * NP), :] for f in range(FIELDS)]
            gy = [g[turn % 2, f, span(size + j * NP), :] for f in range(FIELDS)]
            gz = [gz_at[span(f * NODES + at), :] for f in range(FIELDS)]
            u = [v[span(m * NODES + at), :] for m in range(3)]
            a = u if group == 0 else [flow[span(m * NODES + at), :] for m in range(3)]
            carried = [a[0] * gx[f] + a[1] * gy[f] + a[2] * gz[f] for f in range(FIELDS)]
            weight = -w[span(at), :]
            press = (gx[3], gy[3], gz[3])
            for m in range(3):
                put_layers(wr, FIELDS, m * NODES + at, weight * (carried[m] + press[m]))
            total = weight * (carried[3] + SPEEDS[group] * (gx[0] + gy[1] + gz[2]))
            put_layers(wr, FIELDS, 3 * NODES + at, total)
        for block in range(2 * FIELDS):
            sum_one_plane(wr, block * NODES + base, up, masks)
        if turn == 1:
            sum_inner(wr, FIELDS, up)
        if after is not None and turn >= 1:
            for ready in (0, up) if turn == 1 else (k,):
                after(ready)


def edge_lanes(ref, row, up, size=NP):
    return jnp.concatenate(
        [ref[span(row, size), :LAYER], ref[span(row + up * PLANE, size), LAYER:]], axis=1
    )


def get_edges(ref, row, size=NP):
    return jnp.concatenate(
        [ref[span(row, size), :], ref[span(FIELDS * PLANE + row, size), :]], axis=1
    )


def put_edges(ref, row, value):
    size = value.shape[0]
    ref[span(row, size), :] = value[:, :LAYER]
    ref[span(FIELDS * PLANE + row, size), :] = value[:, LAYER:]


def edge_stage(group, mat, v, vb, w, flow, g, up_out, down_out):
    points = POINTS[group]
    up = points - 1
    d = CONSTS["derivs"][group]
    size = points * NP
    for f in range(FIELDS):
        high, low = split(get_edges(vb, f * PLANE, size))
        g[f, : 2 * size, :] = dot(mat[...], jnp.concatenate([high, low, high], axis=0))
    for j in range(points):
        u = [get_edges(vb, f * PLANE + j * NP) for f in range(FIELDS)]
        gx = [g[f, span(j * NP), :] for f in range(FIELDS)]
        gy = [g[f, span(size + j * NP), :] for f in range(FIELDS)]
        gz = []
        for f in range(FIELDS):
            low = z_derivative(d, 0, range(1, points), v, f, j, slice(0, LAYER))
            high = z_derivative(d, up, range(up), v, f, j, slice(LAYER, 2 * LAYER))
            low = low + float(d[0, 0]) * u[f][:, :LAYER]
            high = high + float(d[up, up]) * u[f][:, LAYER:]
            gz.append(jnp.concatenate([low, high], axis=1))
        a = u if group == 0 else [edge_lanes(flow, m * NODES + j * NP, up) for m in range(3)]
        weight = -edge_lanes(w, j * NP, up)
        carried = [a[0] * gx[f] + a[1] * gy[f] + a[2] * gz[f] for f in range(FIELDS)]
        press = (gx[3], gy[3], gz[3])
        values = [weight * (carried[m] + press[m]) for m in range(3)]
        values.append(weight * (carried[3] + SPEEDS[group] * (gx[0] + gy[1] + gz[2])))
        for f in range(FIELDS):
            down_out[span(f * PLANE + j * NP), :] = values[f][:, :LAYER]
            up_out[span(f * PLANE + j * NP), :] = values[f][:, LAYER:]
    masks = lane_masks()
    sum_in_plane(up_out, FIELDS, up, masks)
    sum_in_plane(down_out, FIELDS, up, masks)


def take_edges(group, ref, out):
    for f in range(FIELDS):
        put_edges(out, f * PLANE, edge_lanes(ref, f * NODES, POINTS[group] - 1, PLANE))


def each_group(ids, body):
    for group in range(2):
        pl.when(ids[0] == group)(lambda group=group: body(group))


def columns(row_table):
    cap, peers = row_table.shape
    tile = jnp.concatenate([row_table, jnp.zeros((cap, LAYER - peers), f32)], axis=1)
    tile = jnp.concatenate([tile, jnp.zeros((NP - cap, LAYER), f32)], axis=0)
    return jnp.transpose(tile)[:peers, :]


def targets(recv, count):
    slot = lax.broadcasted_iota(jnp.int32, recv.shape, 0)
    return jnp.where(slot < count[...], recv[...], -1).astype(f32)


def weights(group, jac, planes):
    wts = np.ones(NP)
    wts[: POINTS[group]] = CONSTS["weights"][group]
    sub = lax.broadcasted_iota(jnp.int32, (NP, 2 * LAYER), 0)
    wi = jnp.zeros((NP, 2 * LAYER), f32)
    for i in range(NP):
        wi = jnp.where(sub == i, float(wts[i]), wi)
    for k in planes:
        for j in range(NP):
            at = k * PLANE + j * NP
            yield k, j, at, (wi * float(wts[k] * wts[j])) * jac[span(at), :]


def first_kernel(
    ids, state, jac, flow, les_mat, ape_mat,
    wr_out, w_out, qw_out, g, gz,
):
    def body(group):
        up = POINTS[group] - 1
        for k, j, at, value in weights(group, jac, range(NP)):
            w_out[span(at), :] = value
            put_layers(qw_out, 1, at, value)
        sum_in_plane(qw_out, 2 * NP, up, lane_masks())
        sum_inner(qw_out, 1, up)
        inner_stage(group, (les_mat, ape_mat)[group], state, w_out, flow, g, gz, wr_out)

    each_group(ids, body)


def flow_copies(flow_at, flow, up, sems):
    copies = []
    for m in range(3):
        for side in range(2):
            where = (
                span(m * NODES + side * up * PLANE, PLANE),
                slice(side * LAYER, (side + 1) * LAYER),
            )
            copies.append(
                pltpu.make_async_copy(flow_at.at[where], flow.at[where], sems.at[2 * m + side])
            )
    return copies


def edge_kernel(
    ids, state, jac, flow_at, les_mat, ape_mat, recv, count,
    up_out, down_out,
    flow, g, w, vb, sems,
):
    cap, peers = recv.shape

    def body(group):
        up = POINTS[group] - 1
        copies = flow_copies(flow_at, flow, up, sems) if group == 1 else []
        for copy in copies:
            copy.start()
        at = span((FIELDS + 1) * PLANE, NP)
        up_out[at, :] = jnp.zeros((NP, LAYER), f32)
        down_out[at, :] = jnp.zeros((NP, LAYER), f32)
        at = span((FIELDS + 1) * PLANE, cap)
        target = targets(recv, count)
        up_out[at, 0:peers] = target
        down_out[at, 0:peers] = target
        for k, j, at, value in weights(group, jac, (0, up)):
            w[span(at), :] = value
        take_edges(group, state, vb)
        at = span(FIELDS * PLANE, PLANE)
        up_out[at, :] = w[span(up * PLANE, PLANE), LAYER:]
        down_out[at, :] = w[span(0, PLANE), :LAYER]
        for copy in copies:
            copy.wait()
        edge_stage(group, (les_mat, ape_mat)[group], state, vb, w, flow, g, up_out, down_out)

    each_group(ids, body)


def block_kernel(
    ids, state, les_at, interp_at, send_at,
    block_out,
    v, les_mat, interp, send, g, lamb, comp, sems,
):
    cap, peers = send.shape

    @pl.when(ids[0] == 0)
    def _():
        copies = [
            pltpu.make_async_copy(les_at, les_mat, sems.at[0]),
            pltpu.make_async_copy(send_at, send, sems.at[1]),
            pltpu.make_async_copy(interp_at, interp, sems.at[2]),
        ]
        fields = [
            pltpu.make_async_copy(
                state.at[span(half * NODES // 2, NODES // 2), :],
                v.at[span(half * NODES // 2, NODES // 2), :],
                sems.at[3 + half],
            )
            for half in range(6)
        ]
        for copy in fields + copies:
            copy.start()
        comp[3 * COMP : EDGE_LO, :] = jnp.zeros((EDGE_LO - 3 * COMP, 2 * LAYER), f32)
        comp[EDGE_LO + 3 * EDGE : EDGE_HI, :] = jnp.zeros((8, 2 * LAYER), f32)
        comp[EDGE_HI + 3 * EDGE : BLOCK, :] = jnp.zeros((8, 2 * LAYER), f32)
        copies[0].wait()
        for copy in fields:
            copy.wait()
        d = CONSTS["derivs"][0]
        for k in range(NP):
            base = k * PLANE
            for f in range(3):
                high, low = split(v[span(f * NODES + base, PLANE), :])
                stack = jnp.concatenate([high, low, high], axis=0)
                some = (slice(PLANE, 2 * PLANE), slice(0, PLANE), slice(0, 2 * PLANE))[f]
                g[k % 2, f, some, :] = dot(les_mat[some, :], stack)
            for j in range(NP):
                at = base + j * NP
                gx = [None] + [g[k % 2, f, span(j * NP), :] for f in (1, 2)]
                gy = [g[k % 2, f, span(PLANE + j * NP), :] for f in (0, 2)]
                gz = [z_derivative(d, k, range(NP), v, f, j) for f in (0, 1)]
                u = [v[span(m * NODES + at), :] for m in range(3)]
                vx = gy[1] - gz[1]
                vy = gz[0] - gx[2]
                vz = gx[1] - gy[0]
                lamb[span(at), :] = vy * u[2] - vz * u[1]
                lamb[span(NODES + at), :] = vz * u[0] - vx * u[2]
                lamb[span(2 * NODES + at), :] = vx * u[1] - vy * u[0]
        copies[1].wait()
        copies[2].wait()
        for m in range(3):
            high, low = split(lamb[m * NODES : (m + 1) * NODES, :])
            got = dot(interp[0], high) + dot(interp[0], low) + dot(interp[1], high)
            comp[m * COMP : (m + 1) * COMP, :] = got[:COMP]
            comp[EDGE_LO + m * EDGE : EDGE_LO + (m + 1) * EDGE, :] = got[COMP : COMP + EDGE]
            comp[EDGE_HI + m * EDGE : EDGE_HI + (m + 1) * EDGE, :] = got[COMP + EDGE :]
        elem = lax.broadcasted_iota(jnp.int32, (peers, 2 * LAYER), 1)
        high, low = split(comp[...])
        table = columns(send[...].astype(f32)).astype(jnp.int32)
        pick = [(table[:, c : c + 1] == elem).astype(f32).astype(bf16) for c in range(cap)]
        pick = jnp.concatenate(pick, axis=0)
        got = dot_nt(pick, high) + dot_nt(pick, low)
        for c in range(cap):
            for t in range(TILES):
                value = got[span(c * peers, peers), t * LAYER : (t + 1) * LAYER]
                if t >= TILES - 2:
                    value = pltpu.roll(value, peers - 1 if t == TILES - 2 else 1, 0)
                block_out[pl.ds(t * cap + c, peers, stride=TILES * cap), :] = value


def add_planes(wr, up, from_below, from_above, fields):
    for f in range(fields):
        at = span(f * PLANE, PLANE)
        lo_rows = span(f * NODES, PLANE)
        hi_rows = span((fields + f) * NODES + up * PLANE, PLANE)
        wr[lo_rows, :] = wr[lo_rows, :] + from_below[at, :]
        wr[hi_rows, :] = wr[hi_rows, :] + from_above[at, :]


def pick_sum(blocks, table, cap, lanes):
    elem = lax.broadcasted_iota(jnp.int32, (table.shape[0], 2 * LAYER), 1).astype(f32)
    pick = [(table[:, c : c + 1] == elem)[:, lanes].astype(f32).astype(bf16) for c in range(cap)]
    high, low = split(jnp.transpose(blocks))
    pick = jnp.concatenate(pick, axis=0)
    return dot(high, pick) + dot(low, pick)


def summed(group, wr, f, k, size, from_below, from_above):
    at = f * NODES + k * PLANE
    low = wr[span(at, size), :]
    high = wr[span(FIELDS * NODES + at, size), :]
    if from_below is not None and k == 0:
        low = low + from_below[span(f * PLANE, size), :]
    if from_above is not None and k == POINTS[group] - 1:
        high = high + from_above[span(f * PLANE, size), :]
    return jnp.concatenate([low, high], axis=1)


def update(
    group, half, state, wr, inv, v, step, acc_in, acc_out, share, from_below, from_above, planes=None
):
    for k in range(POINTS[group]) if planes is None else planes:
        size = POINTS[group] * NP
        scale = get_layers(inv, 1, k * PLANE, size)
        for f in range(FIELDS):
            at = f * NODES + k * PLANE
            rate = summed(group, wr, f, k, size, from_below, from_above) * scale
            base = half[span(at, size), :]
            if acc_in is None or step == time_step:
                full = base + (base - state[span(at, size), :])
            if step == time_step:
                base = full
            v[span(at, size), :] = base + step * rate
            before = full if acc_in is None else acc_in[span(at, size), :]
            acc_out[span(at, size), :] = before + share * rate


def second_kernel(
    ids, block, recv, count, from_below, from_above, state, w, qw, flow_at, les_mat, ape_mat, place,
    place_edge, wr_in,
    v, inv_out, acc_out, half_out, acc_edges, up_out, down_out, g, vb, src, edge, flow, sems,
):
    cap, peers = recv.shape
    weights_at = span(FIELDS * PLANE, PLANE)

    def source():
        up = NA - 1
        masks = lane_masks()
        tiles = []
        for t in range(TILES):
            parts = [
                block[pl.ds(t * cap + c, peers, stride=TILES * cap), :] for c in range(cap)
            ]
            tiles.append(jnp.concatenate(parts, axis=0))
        tables_at = span((FIELDS + 1) * PLANE, cap)
        own = columns(targets(recv, count))
        below = columns(from_below[tables_at, 0:peers])
        above = columns(from_above[tables_at, 0:peers])
        own = pick_sum(
            jnp.concatenate(tiles[: TILES - 2], axis=1), own, cap, slice(0, 2 * LAYER)
        )
        lo_edge = pick_sum(tiles[TILES - 2], above, cap, slice(0, LAYER))
        hi_edge = pick_sum(tiles[TILES - 1], below, cap, slice(LAYER, 2 * LAYER))
        for m in range(3):
            high, low = split(own[m * COMP : (m + 1) * COMP])
            full = dot(place[...], jnp.concatenate([high, low], axis=0))
            size = NA * PLANE
            put_layers(src, 3, m * NODES, full * w[0:size, :])
            high, low = split(hi_edge[m * EDGE : (m + 1) * EDGE])
            full = dot(place_edge[...], jnp.concatenate([high, low], axis=0))
            edge[span(m * PLANE, PLANE), :] = full * from_below[weights_at, :]
            high, low = split(lo_edge[m * EDGE : (m + 1) * EDGE])
            full = dot(place_edge[...], jnp.concatenate([high, low], axis=0))
            edge[span((3 + m) * PLANE, PLANE), :] = full * from_above[weights_at, :]
        sum_in_plane(src, 6 * NP, up, masks)
        sum_in_plane(edge, 6, up, masks)
        sum_inner(src, 3, up)
        add_planes(src, up, edge.at[0 : 3 * PLANE], edge.at[3 * PLANE : 6 * PLANE], 3)
        size = NA * NP
        for k in range(NA):
            scale = (0.5 * time_step) * get_layers(inv_out, 1, k * PLANE, size)
            for f in range(FIELDS):
                at = f * NODES + k * PLANE
                value = state[span(at, size), :]
                if f < 3:
                    value = value + scale * get_layers(src, 3, at, size)
                half_out[span(at, size), :] = value

    def body(group):
        up = POINTS[group] - 1
        copies = flow_copies(flow_at, flow, up, sems) if group == 1 else []
        for copy in copies:
            copy.start()
        inv_out[...] = qw[...]
        edge[0:PLANE, :] = from_below[weights_at, :]
        edge[PLANE : 2 * PLANE, :] = from_above[weights_at, :]
        sum_in_plane(edge, 2, up, lane_masks())
        add_planes(inv_out, up, edge.at[0:PLANE], edge.at[PLANE : 2 * PLANE], 1)
        inv_out[...] = 1.0 / inv_out[...]
        if group == 1:
            source()
        else:
            half_out[...] = state[...]
        update(group, half_out, state, wr_in, inv_out, v, 0.5 * time_step, None, acc_out,
               time_step / 6.0, from_below, from_above)
        take_edges(group, v, vb)
        take_edges(group, acc_out, acc_edges)
        for copy in copies:
            copy.wait()
        edge_stage(group, (les_mat, ape_mat)[group], v, vb, w, flow, g, up_out, down_out)

    each_group(ids, body)


def edge_rate(group, f, from_below, from_above, down, up_planes, inv):
    size = POINTS[group] * NP
    at = span(f * PLANE, size)
    low = down[at, :] + from_below[at, :]
    high = up_planes[at, :] + from_above[at, :]
    low = low * inv[span(0, size), :]
    high = high * inv[span(NODES + (POINTS[group] - 1) * PLANE, size), :]
    return jnp.concatenate([low, high], axis=1)


def edge_step_kernel(
    step, ids, from_below, from_above, down, up_planes, v, half, state, w, inv, flow, les_mat,
    ape_mat, acc_in,
    vb, acc_edges, up_out, down_out, g,
):
    def body(group):
        up = POINTS[group] - 1
        size = POINTS[group] * NP
        for f in range(FIELDS):
            rate = edge_rate(group, f, from_below, from_above, down, up_planes, inv)
            base = edge_lanes(half, f * NODES, up, size)
            if step == time_step:
                base = base + (base - edge_lanes(state, f * NODES, up, size))
            put_edges(vb, f * PLANE, base + step * rate)
            before = get_edges(acc_in, f * PLANE, size)
            put_edges(acc_edges, f * PLANE, before + (time_step / 3.0) * rate)
        edge_stage(group, (les_mat, ape_mat)[group], v, vb, w, flow, g, up_out, down_out)

    each_group(ids, body)


def inner_kernel(step, ids, v_in, *refs):
    if step == 0.5 * time_step:
        half, state, w, inv, flow, les_mat, ape_mat, acc_in, v_out, acc_out, g, gz, wr = refs
        v = v_in
    else:
        vb, half, state, w, inv, flow, les_mat, ape_mat, acc_in = refs[:9]
        if step is None:
            acc_out, g, gz, wr, v, result, sems = refs[9:]
        else:
            v_out, acc_out, g, gz, wr, v = refs[9:]

    def body(group):
        if v is not v_in:
            v[...] = v_in[...]
            for f in range(FIELDS):
                size = POINTS[group] * NP
                up = POINTS[group] - 1
                value = get_edges(vb, f * PLANE, size)
                v[span(f * NODES, size), :LAYER] = value[:, :LAYER]
                v[span(f * NODES + up * PLANE, size), LAYER:] = value[:, LAYER:]
        copies = []

        def after(k):
            if step is None:
                finish(group, wr, inv, acc_in, result, k)
                send_out(k)
            else:
                update(group, half, state, wr, inv, v_out, step, acc_in, acc_out, time_step / 3.0,
                       None, None, (k,))

        def send_out(k):
            for f in range(FIELDS):
                at = span(f * NODES + k * PLANE, PLANE)
                copy = pltpu.make_async_copy(
                    result.at[at, :], acc_out.at[at, :], sems.at[k * FIELDS + f]
                )
                copy.start()
                copies.append(copy)

        if step is None:
            for k in range(POINTS[group], NP):
                finish(group, wr, inv, acc_in, result, k)
                send_out(k)
        inner_stage(group, (les_mat, ape_mat)[group], v, w, flow, g, gz, wr, after)
        for copy in copies:
            copy.wait()

    each_group(ids, body)


def finish(group, wr, inv, acc_in, out, k):
    points = POINTS[group]
    size = points * NP
    keep = lax.broadcasted_iota(jnp.int32, (size, 2 * LAYER), 0) % NP < points
    for f in range(FIELDS):
        at = f * NODES + k * PLANE
        done = 0
        if k < points:
            scale = get_layers(inv, 1, k * PLANE, size) * (time_step / 6.0)
            rate = summed(group, wr, f, k, size, None, None) * scale
            value = acc_in[span(at, size), :] + rate
            if points < NP:
                value = jnp.where(keep, value, 0.0)
            out[span(at, size), :] = value
            done = size
        if done < PLANE:
            out[span(at + done, PLANE - done), :] = jnp.zeros((PLANE - done, 2 * LAYER), f32)


def last_kernel(
    ids, from_below, from_above, down, up_planes, inv, acc_edges, inner, out, planes, sems
):
    def body(group):
        points = POINTS[group]
        size = points * NP
        keep = lax.broadcasted_iota(jnp.int32, (size, 2 * LAYER), 0) % NP < points
        copies = []
        for f in range(FIELDS):
            rate = edge_rate(group, f, from_below, from_above, down, up_planes, inv)
            value = get_edges(acc_edges, f * PLANE, size) + (time_step / 6.0) * rate
            if points < NP:
                value = jnp.where(keep, value, 0.0)
            put_edges(planes, f * PLANE, value)
            for side in range(2):
                row = f * NODES + side * (points - 1) * PLANE
                copies.append(
                    pltpu.make_async_copy(
                        planes.at[span((side * FIELDS + f) * PLANE, size), :],
                        out.at[span(row, size), side * LAYER : (side + 1) * LAYER],
                        sems.at[side * FIELDS + f],
                    )
                )
                copies[-1].start()
        for copy in copies:
            copy.wait()

    each_group(ids, body)


SMEM = pl.BlockSpec(memory_space=pltpu.SMEM)
VMEM = pl.BlockSpec(memory_space=pltpu.VMEM)


def call(kernel, args, outs, scratch, megabytes):
    return pl.pallas_call(
        kernel,
        out_shape=[jax.ShapeDtypeStruct(s, f32) for s in outs],
        in_specs=[SMEM] + [VMEM] * (len(args) - 1),
        out_specs=[VMEM] * len(outs),
        scratch_shapes=[pltpu.VMEM(s, f32) for s in scratch],
        compiler_params=pltpu.CompilerParams(vmem_limit_bytes=megabytes * 1024 * 1024),
    )(*args)


def on_device(state, mean_flow, jacobian, send_elem, recv_elem, recv_count):
    ids = lax.axis_index("grp").astype(jnp.int32).reshape(1)
    width = state.shape[-1]
    peers, cap = send_elem.shape[1:]
    state = state.reshape(FIELDS * NODES, width)
    flow = mean_flow.reshape(3 * NODES, width)
    jac = jacobian.reshape(NODES, width)
    send = jnp.swapaxes(send_elem, 1, 2).reshape(cap, peers)
    recv = jnp.swapaxes(recv_elem, 1, 2).reshape(cap, peers)
    les_mat, ape_mat = (jnp.asarray(m) for m in CONSTS["mats"])
    interp = jnp.asarray(CONSTS["interp"])
    place = jnp.asarray(CONSTS["place"])
    place_edge = jnp.asarray(CONSTS["place_edge"])
    full = (FIELDS * NODES, width)
    one = (NODES, width)
    layered = (2 * FIELDS * NODES, LAYER)
    one_layered = (2 * NODES, LAYER)
    thin = (FIELDS * PLANE, LAYER)
    edges = (2 * FIELDS * PLANE, LAYER)
    thick = ((FIELDS + 1) * PLANE + NP, LAYER)
    grads = (2, FIELDS, 2 * PLANE, width)
    size = lax.axis_size("elem")
    up_pairs = [(i, (i + 1) % size) for i in range(size)]
    down_pairs = [(j, i) for i, j in up_pairs]

    def exchange(up_planes, down_planes):
        return (
            lax.ppermute(up_planes, "elem", up_pairs),
            lax.ppermute(down_planes, "elem", down_pairs),
        )

    hbm = pl.BlockSpec(memory_space=pltpu.HBM)
    (block,) = pl.pallas_call(
        block_kernel,
        out_shape=[jax.ShapeDtypeStruct((TILES * cap * peers, LAYER), f32)],
        in_specs=[SMEM] + [hbm] * 4,
        out_specs=[VMEM],
        scratch_shapes=[
            pltpu.VMEM((3 * NODES, width), f32),
            pltpu.VMEM(les_mat.shape, bf16),
            pltpu.VMEM(interp.shape, bf16),
            pltpu.VMEM((cap, peers), jnp.int32),
            pltpu.VMEM(grads, f32),
            pltpu.VMEM((3 * NODES, width), f32),
            pltpu.VMEM((BLOCK, width), f32),
            pltpu.SemaphoreType.DMA((9,)),
        ],
        compiler_params=pltpu.CompilerParams(vmem_limit_bytes=62 * 1024 * 1024),
    )(ids, state, les_mat, interp, send)
    up_planes, down_planes = pl.pallas_call(
        edge_kernel,
        out_shape=[jax.ShapeDtypeStruct(thick, f32)] * 2,
        in_specs=[SMEM] + [VMEM] * 2 + [hbm] + [VMEM] * 4,
        out_specs=[VMEM] * 2,
        scratch_shapes=[
            pltpu.VMEM((3 * NODES, width), f32),
            pltpu.VMEM(grads[1:], f32),
            pltpu.VMEM(one, f32),
            pltpu.VMEM(edges, f32),
            pltpu.SemaphoreType.DMA((6,)),
        ],
        compiler_params=pltpu.CompilerParams(vmem_limit_bytes=8 * 1024 * 1024),
    )(ids, state, jac, flow, les_mat, ape_mat, recv, recv_count)
    from_below, from_above = exchange(up_planes, down_planes)
    block = lax.all_to_all(block, "elem", split_axis=0, concat_axis=0, tiled=True)
    block, from_below, from_above, late_ids = lax.optimization_barrier(
        (block, from_below, from_above, ids)
    )
    wr, w, qw = call(
        first_kernel,
        (late_ids, state, jac, flow, les_mat, ape_mat),
        [layered, one, one_layered],
        [grads, full],
        12,
    )
    block = lax.ppermute(block, "grp", [(0, 1)])
    v, inv, acc, half, acc_edges, up_planes, down_planes = pl.pallas_call(
        second_kernel,
        out_shape=[
            jax.ShapeDtypeStruct(s, f32)
            for s in (full, one_layered, full, full, edges, thin, thin)
        ],
        in_specs=[SMEM] + [VMEM] * 8 + [hbm] + [VMEM] * 5,
        out_specs=[VMEM] * 7,
        scratch_shapes=[
            pltpu.VMEM(s, f32)
            for s in (grads[1:], edges, (6 * NODES, LAYER), (6 * PLANE, LAYER), (3 * NODES, width))
        ]
        + [pltpu.SemaphoreType.DMA((6,))],
        compiler_params=pltpu.CompilerParams(vmem_limit_bytes=24 * 1024 * 1024),
    )(
        ids, block, recv, recv_count, from_below, from_above, state, w, qw, flow, les_mat,
        ape_mat, place, place_edge, wr,
    )
    vb = None
    for step in (0.5 * time_step, time_step, None):
        from_below, from_above = exchange(up_planes, down_planes)

        def inner(*refs, step=step):
            inner_kernel(step, *refs)

        def edge_step(*refs, step=step):
            edge_step_kernel(step, *refs)

        rest = (half, state, w, inv, flow, les_mat, ape_mat, acc)
        if vb is None:
            v, acc = call(inner, (ids, v) + rest, [full, full], [grads, full, layered], 24)
        elif step is not None:
            v, acc = call(inner, (ids, v, vb) + rest, [full, full], [grads, full, layered, full], 24)
        else:
            out = pl.pallas_call(
                inner,
                out_shape=jax.ShapeDtypeStruct(full, f32),
                in_specs=[SMEM] + [VMEM] * 10,
                out_specs=hbm,
                scratch_shapes=[pltpu.VMEM(s, f32) for s in (grads, full, layered, full, full)]
                + [pltpu.SemaphoreType.DMA((FIELDS * NP,))],
                compiler_params=pltpu.CompilerParams(vmem_limit_bytes=24 * 1024 * 1024),
            )(ids, v, vb, *rest)
            break
        vb, acc_edges, up_planes, down_planes = call(
            edge_step,
            (ids, from_below, from_above, down_planes, up_planes, v, half, state, w, inv, flow,
             les_mat, ape_mat, acc_edges),
            [edges, edges, thin, thin],
            [grads[1:]],
            14,
        )
    out = pl.pallas_call(
        last_kernel,
        out_shape=jax.ShapeDtypeStruct(full, f32),
        in_specs=[SMEM] + [VMEM] * 6 + [hbm],
        out_specs=hbm,
        scratch_shapes=[pltpu.VMEM(edges, f32), pltpu.SemaphoreType.DMA((2 * FIELDS,))],
        input_output_aliases={7: 0},
        compiler_params=pltpu.CompilerParams(vmem_limit_bytes=6 * 1024 * 1024),
    )(ids, from_below, from_above, down_planes, up_planes, inv, acc_edges, out)
    return out.reshape(1, FIELDS, NODES, width)


def solution(mesh):
    placed = (
        P("grp", None, None, "elem"),
        P(None, None, "elem"),
        P("grp", None, "elem"),
        P("elem", None, None),
        P("elem", None, None),
        P("elem", None),
    )
    return jax.shard_map(
        on_device,
        mesh=mesh,
        in_specs=placed,
        out_specs=P("grp", None, None, "elem"),
        check_vma=False,
    )
```

```python
import jax
import jax.numpy as jnp
import numpy as np
from jax import lax
from jax.experimental import pallas as pl
from jax.experimental.pallas import tpu as pltpu
from jax.sharding import PartitionSpec as P

NP = 8
NA = 6
EX = 16
EY = 8
LAYER = EX * EY
NODES = NP**3
PLANE = NP * NP
FIELDS = 4
COMP = NA**3
EDGE = 40
BLOCK = 1024
TILES = BLOCK // LAYER
EDGE_LO = 768
EDGE_HI = 896

les_speed_sq = 9.0
ape_speed_sq = 4.0
time_step = 0.004
f32 = jnp.float32
bf16 = jnp.bfloat16


def legendre_pair(points, node_pos):
    degree = points - 1
    before = np.ones(node_pos.shape[0])
    current = node_pos.copy()
    for order in range(2, degree + 1):
        after = ((2 * order - 1) * node_pos * current - (order - 1) * before) / order
        before = current
        current = after
    return (current, before)


def lobatto_tables(points):
    degree = points - 1
    node_pos = -np.cos(np.pi * np.arange(points) / degree)
    for sweep in range(100):
        top_vals, prev_vals = legendre_pair(points, node_pos)
        node_pos = node_pos - (node_pos * top_vals - prev_vals) / (points * top_vals)
    node_pos[0] = -1.0
    node_pos[points - 1] = 1.0
    node_vals, unused_vals = legendre_pair(points, node_pos)
    weights = 2.0 / (points * (points - 1) * node_vals**2)
    derivative = np.zeros((points, points))
    for target in range(points):
        for source in range(points):
            if target != source:
                derivative[target, source] = node_vals[target] / (
                    node_vals[source] * (node_pos[target] - node_pos[source])
                )
    derivative[0, 0] = -points * (points - 1) / 4.0
    derivative[points - 1, points - 1] = points * (points - 1) / 4.0
    return (node_pos, weights, derivative)


def split_np(table):
    high = table.astype(np.float32).astype(jnp.bfloat16)
    low = (table - high.astype(np.float64)).astype(np.float32).astype(jnp.bfloat16)
    return high, low


def tables():
    les_pos, les_wts, les_deriv = lobatto_tables(NP)
    ape_pos, ape_wts, ape_deriv = lobatto_tables(NA)
    mats = []
    for points, deriv in ((NP, les_deriv), (NA, ape_deriv)):
        wide = np.zeros((NP, NP))
        wide[:points, :points] = deriv
        both = np.concatenate(
            [np.kron(np.eye(points), wide), np.kron(deriv, np.eye(NP))], axis=0
        )
        high, low = split_np(both)
        mats.append(np.concatenate([high, high, low], axis=1))
    lagrange = np.ones((NA, NP))
    for target in range(NA):
        for source in range(NP):
            for pivot_id in range(NP):
                if pivot_id != source:
                    lagrange[target, source] *= (ape_pos[target] - les_pos[pivot_id]) / (
                        les_pos[source] - les_pos[pivot_id]
                    )
    compact = np.kron(lagrange, np.kron(lagrange, lagrange))
    interp = np.zeros((COMP + 2 * EDGE, NODES))
    interp[:COMP] = compact
    interp[COMP : COMP + NA * NA] = compact[: NA * NA]
    interp[COMP + EDGE : COMP + EDGE + NA * NA] = compact[COMP - NA * NA :]
    high, low = split_np(interp)
    place = np.zeros((NA * PLANE, COMP))
    for slot in range(COMP):
        k, j, i = slot // (NA * NA), slot // NA % NA, slot % NA
        place[(k * NP + j) * NP + i, slot] = 1.0
    place_edge = np.zeros((PLANE, EDGE))
    place_edge[:, : NA * NA] = place[:PLANE, : NA * NA]
    return dict(
        derivs=(les_deriv, ape_deriv),
        weights=(les_wts, ape_wts),
        mats=mats,
        interp=np.stack([high, low]),
        place=np.concatenate([place, place], axis=1).astype(jnp.bfloat16),
        place_edge=np.concatenate([place_edge, place_edge], axis=1).astype(jnp.bfloat16),
    )


CONSTS = tables()
POINTS = (NP, NA)
SPEEDS = (les_speed_sq, ape_speed_sq)


def dot(a, b):
    return lax.dot_general(a, b, (((1,), (0,)), ((), ())), preferred_element_type=f32)


def dot_nt(a, b):
    return lax.dot_general(a, b, (((1,), (1,)), ((), ())), preferred_element_type=f32)


def split(x):
    high = x.astype(bf16)
    return high, (x - high.astype(f32)).astype(bf16)


def lane_masks():
    lane = lax.broadcasted_iota(jnp.int32, (1, LAYER), 1)
    east = lane % EX
    return (
        (east > 0).astype(f32),
        (east < EX - 1).astype(f32),
        (lane >= EX).astype(f32),
        (lane < LAYER - EX).astype(f32),
    )


def pair_sum(lo, hi, stride, has_prev, has_next):
    return (
        lo + pltpu.roll(hi, stride, 1) * has_prev,
        hi + pltpu.roll(lo, LAYER - stride, 1) * has_next,
    )


def sum_one_plane(ref, row, up, masks):
    px, nx, py, ny = masks
    lo_at = pl.ds(row, NP, stride=NP)
    hi_at = pl.ds(row + up, NP, stride=NP)
    lo, hi = pair_sum(ref[lo_at, :], ref[hi_at, :], 1, px, nx)
    ref[lo_at, :] = lo
    ref[hi_at, :] = hi
    lo_rows = span(row)
    hi_rows = span(row + up * NP)
    lo, hi = pair_sum(ref[lo_rows, :], ref[hi_rows, :], EX, py, ny)
    ref[lo_rows, :] = lo
    ref[hi_rows, :] = hi


def sum_in_plane(ref, blocks, up, masks):
    for block in range(blocks):
        sum_one_plane(ref, block * PLANE, up, masks)


def sum_inner(ref, fields, up):
    for f in range(fields):
        hi_rows = span(f * NODES + up * PLANE, PLANE)
        lo_rows = span((fields + f) * NODES, PLANE)
        both = ref[hi_rows, :] + ref[lo_rows, :]
        ref[hi_rows, :] = both
        ref[lo_rows, :] = both


def span(start, size=NP):
    return slice(start, start + size)


def put_layers(ref, fields, row, value):
    size = value.shape[0]
    ref[span(row, size), :] = value[:, :LAYER]
    ref[span(fields * NODES + row, size), :] = value[:, LAYER:]


def get_layers(ref, fields, row, size):
    return jnp.concatenate(
        [ref[span(row, size), :], ref[span(fields * NODES + row, size), :]], axis=1
    )


def z_derivative(d, k, planes, v, f, j, lanes=slice(None)):
    total = None
    for q in planes:
        if d[k, q] != 0.0:
            part = float(d[k, q]) * v[span(f * NODES + q * PLANE + j * NP), lanes]
            total = part if total is None else total + part
    return total


def z_derivatives(d, points, v, gz):
    for f in range(FIELDS):
        for j in range(points):
            at = [f * NODES + q * PLANE + j * NP for q in range(points)]
            u = [v[span(a), :] for a in at]
            half = points // 2
            even = [u[q] + u[points - 1 - q] for q in range(half)]
            odd = [u[q] - u[points - 1 - q] for q in range(half)]
            for k in range(half):
                first = second = None
                for q in range(half):
                    x = float(0.5 * (d[k, q] + d[k, points - 1 - q])) * even[q]
                    y = float(0.5 * (d[k, q] - d[k, points - 1 - q])) * odd[q]
                    first = x if first is None else first + x
                    second = y if second is None else second + y
                gz[span(at[k]), :] = second + first
                gz[span(at[points - 1 - k]), :] = second - first


def inner_stage(group, mat, v, w, flow, g, gz_at, wr, after=None):
    points = POINTS[group]
    up = points - 1
    d = CONSTS["derivs"][group]
    size = points * NP
    masks = lane_masks()
    z_derivatives(d, points, v, gz_at)
    for turn, k in enumerate([0, up] + list(range(1, up))):
        base = k * PLANE
        for f in range(FIELDS):
            high, low = split(v[span(f * NODES + base, size), :])
            g[turn % 2, f, : 2 * size, :] = dot(mat[...], jnp.concatenate([high, low, high], axis=0))
        for j in range(points):
            at = base + j * NP
            gx = [g[turn % 2, f, span(j * NP), :] for f in range(FIELDS)]
            gy = [g[turn % 2, f, span(size + j * NP), :] for f in range(FIELDS)]
            gz = [gz_at[span(f * NODES + at), :] for f in range(FIELDS)]
            u = [v[span(m * NODES + at), :] for m in range(3)]
            a = u if group == 0 else [flow[span(m * NODES + at), :] for m in range(3)]
            carried = [a[0] * gx[f] + a[1] * gy[f] + a[2] * gz[f] for f in range(FIELDS)]
            weight = -w[span(at), :]
            press = (gx[3], gy[3], gz[3])
            for m in range(3):
                put_layers(wr, FIELDS, m * NODES + at, weight * (carried[m] + press[m]))
            total = weight * (carried[3] + SPEEDS[group] * (gx[0] + gy[1] + gz[2]))
            put_layers(wr, FIELDS, 3 * NODES + at, total)
        for block in range(2 * FIELDS):
            sum_one_plane(wr, block * NODES + base, up, masks)
        if turn == 1:
            sum_inner(wr, FIELDS, up)
        if after is not None and turn >= 1:
            for ready in (0, up) if turn == 1 else (k,):
                after(ready)


def edge_lanes(ref, row, up, size=NP):
    return jnp.concatenate(
        [ref[span(row, size), :LAYER], ref[span(row + up * PLANE, size), LAYER:]], axis=1
    )


def get_edges(ref, row, size=NP):
    return jnp.concatenate(
        [ref[span(row, size), :], ref[span(FIELDS * PLANE + row, size), :]], axis=1
    )


def put_edges(ref, row, value):
    size = value.shape[0]
    ref[span(row, size), :] = value[:, :LAYER]
    ref[span(FIELDS * PLANE + row, size), :] = value[:, LAYER:]


def edge_stage(group, mat, v, vb, w, flow, g, up_out, down_out):
    points = POINTS[group]
    up = points - 1
    d = CONSTS["derivs"][group]
    size = points * NP
    for f in range(FIELDS):
        high, low = split(get_edges(vb, f * PLANE, size))
        g[f, : 2 * size, :] = dot(mat[...], jnp.concatenate([high, low, high], axis=0))
    for j in range(points):
        u = [get_edges(vb, f * PLANE + j * NP) for f in range(FIELDS)]
        gx = [g[f, span(j * NP), :] for f in range(FIELDS)]
        gy = [g[f, span(size + j * NP), :] for f in range(FIELDS)]
        gz = []
        for f in range(FIELDS):
            low = z_derivative(d, 0, range(1, points), v, f, j, slice(0, LAYER))
            high = z_derivative(d, up, range(up), v, f, j, slice(LAYER, 2 * LAYER))
            low = low + float(d[0, 0]) * u[f][:, :LAYER]
            high = high + float(d[up, up]) * u[f][:, LAYER:]
            gz.append(jnp.concatenate([low, high], axis=1))
        a = u if group == 0 else [edge_lanes(flow, m * NODES + j * NP, up) for m in range(3)]
        weight = -edge_lanes(w, j * NP, up)
        carried = [a[0] * gx[f] + a[1] * gy[f] + a[2] * gz[f] for f in range(FIELDS)]
        press = (gx[3], gy[3], gz[3])
        values = [weight * (carried[m] + press[m]) for m in range(3)]
        values.append(weight * (carried[3] + SPEEDS[group] * (gx[0] + gy[1] + gz[2])))
        for f in range(FIELDS):
            down_out[span(f * PLANE + j * NP), :] = values[f][:, :LAYER]
            up_out[span(f * PLANE + j * NP), :] = values[f][:, LAYER:]
    masks = lane_masks()
    sum_in_plane(up_out, FIELDS, up, masks)
    sum_in_plane(down_out, FIELDS, up, masks)


def take_edges(group, ref, out):
    for f in range(FIELDS):
        put_edges(out, f * PLANE, edge_lanes(ref, f * NODES, POINTS[group] - 1, PLANE))


def each_group(ids, body):
    for group in range(2):
        pl.when(ids[0] == group)(lambda group=group: body(group))


def columns(row_table):
    cap, peers = row_table.shape
    tile = jnp.concatenate([row_table, jnp.zeros((cap, LAYER - peers), f32)], axis=1)
    tile = jnp.concatenate([tile, jnp.zeros((NP - cap, LAYER), f32)], axis=0)
    return jnp.transpose(tile)[:peers, :]


def targets(recv, count):
    slot = lax.broadcasted_iota(jnp.int32, recv.shape, 0)
    return jnp.where(slot < count[...], recv[...], -1).astype(f32)


def weights(group, jac, planes):
    wts = np.ones(NP)
    wts[: POINTS[group]] = CONSTS["weights"][group]
    sub = lax.broadcasted_iota(jnp.int32, (NP, 2 * LAYER), 0)
    wi = jnp.zeros((NP, 2 * LAYER), f32)
    for i in range(NP):
        wi = jnp.where(sub == i, float(wts[i]), wi)
    for k in planes:
        for j in range(NP):
            at = k * PLANE + j * NP
            yield k, j, at, (wi * float(wts[k] * wts[j])) * jac[span(at), :]


def first_kernel(
    ids, state, jac, flow, les_mat, ape_mat,
    wr_out, w_out, qw_out, g, gz,
):
    def body(group):
        up = POINTS[group] - 1
        for k, j, at, value in weights(group, jac, range(NP)):
            w_out[span(at), :] = value
            put_layers(qw_out, 1, at, value)
        sum_in_plane(qw_out, 2 * NP, up, lane_masks())
        sum_inner(qw_out, 1, up)
        inner_stage(group, (les_mat, ape_mat)[group], state, w_out, flow, g, gz, wr_out)

    each_group(ids, body)


def flow_copies(flow_at, flow, up, sems):
    copies = []
    for m in range(3):
        for side in range(2):
            where = (
                span(m * NODES + side * up * PLANE, PLANE),
                slice(side * LAYER, (side + 1) * LAYER),
            )
            copies.append(
                pltpu.make_async_copy(flow_at.at[where], flow.at[where], sems.at[2 * m + side])
            )
    return copies


def edge_kernel(
    ids, state, jac, flow_at, les_mat, ape_mat, recv, count,
    up_out, down_out,
    flow, g, w, vb, sems,
):
    cap, peers = recv.shape

    def body(group):
        up = POINTS[group] - 1
        copies = flow_copies(flow_at, flow, up, sems) if group == 1 else []
        for copy in copies:
            copy.start()
        at = span((FIELDS + 1) * PLANE, NP)
        up_out[at, :] = jnp.zeros((NP, LAYER), f32)
        down_out[at, :] = jnp.zeros((NP, LAYER), f32)
        at = span((FIELDS + 1) * PLANE, cap)
        target = targets(recv, count)
        up_out[at, 0:peers] = target
        down_out[at, 0:peers] = target
        for k, j, at, value in weights(group, jac, (0, up)):
            w[span(at), :] = value
        take_edges(group, state, vb)
        at = span(FIELDS * PLANE, PLANE)
        up_out[at, :] = w[span(up * PLANE, PLANE), LAYER:]
        down_out[at, :] = w[span(0, PLANE), :LAYER]
        for copy in copies:
            copy.wait()
        edge_stage(group, (les_mat, ape_mat)[group], state, vb, w, flow, g, up_out, down_out)

    each_group(ids, body)


def block_kernel(
    ids, state, les_at, interp_at, send_at,
    block_out,
    v, les_mat, interp, send, g, lamb, comp, sems,
):
    cap, peers = send.shape

    @pl.when(ids[0] == 0)
    def _():
        copies = [
            pltpu.make_async_copy(les_at, les_mat, sems.at[0]),
            pltpu.make_async_copy(send_at, send, sems.at[1]),
            pltpu.make_async_copy(interp_at, interp, sems.at[2]),
        ]
        fields = [
            pltpu.make_async_copy(
                state.at[span(half * NODES // 2, NODES // 2), :],
                v.at[span(half * NODES // 2, NODES // 2), :],
                sems.at[3 + half],
            )
            for half in range(6)
        ]
        for copy in fields + copies:
            copy.start()
        comp[3 * COMP : EDGE_LO, :] = jnp.zeros((EDGE_LO - 3 * COMP, 2 * LAYER), f32)
        comp[EDGE_LO + 3 * EDGE : EDGE_HI, :] = jnp.zeros((8, 2 * LAYER), f32)
        comp[EDGE_HI + 3 * EDGE : BLOCK, :] = jnp.zeros((8, 2 * LAYER), f32)
        copies[0].wait()
        for copy in fields:
            copy.wait()
        d = CONSTS["derivs"][0]
        for k in range(NP):
            base = k * PLANE
            for f in range(3):
                high, low = split(v[span(f * NODES + base, PLANE), :])
                stack = jnp.concatenate([high, low, high], axis=0)
                some = (slice(PLANE, 2 * PLANE), slice(0, PLANE), slice(0, 2 * PLANE))[f]
                g[k % 2, f, some, :] = dot(les_mat[some, :], stack)
            for j in range(NP):
                at = base + j * NP
                gx = [None] + [g[k % 2, f, span(j * NP), :] for f in (1, 2)]
                gy = [g[k % 2, f, span(PLANE + j * NP), :] for f in (0, 2)]
                gz = [z_derivative(d, k, range(NP), v, f, j) for f in (0, 1)]
                u = [v[span(m * NODES + at), :] for m in range(3)]
                vx = gy[1] - gz[1]
                vy = gz[0] - gx[2]
                vz = gx[1] - gy[0]
                lamb[span(at), :] = vy * u[2] - vz * u[1]
                lamb[span(NODES + at), :] = vz * u[0] - vx * u[2]
                lamb[span(2 * NODES + at), :] = vx * u[1] - vy * u[0]
        copies[1].wait()
        copies[2].wait()
        for m in range(3):
            high, low = split(lamb[m * NODES : (m + 1) * NODES, :])
            size = COMP + 2 * EDGE
            both = dot(interp[...].reshape(2 * size, NODES), high)
            got = both[:size] + both[size:] + dot(interp[0], low)
            comp[m * COMP : (m + 1) * COMP, :] = got[:COMP]
            comp[EDGE_LO + m * EDGE : EDGE_LO + (m + 1) * EDGE, :] = got[COMP : COMP + EDGE]
            comp[EDGE_HI + m * EDGE : EDGE_HI + (m + 1) * EDGE, :] = got[COMP + EDGE :]
        elem = lax.broadcasted_iota(jnp.int32, (peers, 2 * LAYER), 1)
        high, low = split(comp[...])
        table = columns(send[...].astype(f32)).astype(jnp.int32)
        pick = [(table[:, c : c + 1] == elem).astype(f32).astype(bf16) for c in range(cap)]
        pick = jnp.concatenate(pick, axis=0)
        got = dot_nt(pick, high) + dot_nt(pick, low)
        for c in range(cap):
            for t in range(TILES):
                value = got[span(c * peers, peers), t * LAYER : (t + 1) * LAYER]
                if t >= TILES - 2:
                    value = pltpu.roll(value, peers - 1 if t == TILES - 2 else 1, 0)
                block_out[pl.ds(t * cap + c, peers, stride=TILES * cap), :] = value


def add_planes(wr, up, from_below, from_above, fields):
    for f in range(fields):
        at = span(f * PLANE, PLANE)
        lo_rows = span(f * NODES, PLANE)
        hi_rows = span((fields + f) * NODES + up * PLANE, PLANE)
        wr[lo_rows, :] = wr[lo_rows, :] + from_below[at, :]
        wr[hi_rows, :] = wr[hi_rows, :] + from_above[at, :]


def pick_sum(blocks, table, cap, lanes):
    elem = lax.broadcasted_iota(jnp.int32, (table.shape[0], 2 * LAYER), 1).astype(f32)
    pick = [(table[:, c : c + 1] == elem)[:, lanes].astype(f32).astype(bf16) for c in range(cap)]
    high, low = split(jnp.transpose(blocks))
    pick = jnp.concatenate(pick, axis=0)
    return dot(high, pick) + dot(low, pick)


def summed(group, wr, f, k, size, from_below, from_above):
    at = f * NODES + k * PLANE
    low = wr[span(at, size), :]
    high = wr[span(FIELDS * NODES + at, size), :]
    if from_below is not None and k == 0:
        low = low + from_below[span(f * PLANE, size), :]
    if from_above is not None and k == POINTS[group] - 1:
        high = high + from_above[span(f * PLANE, size), :]
    return jnp.concatenate([low, high], axis=1)


def update(
    group, half, state, wr, inv, v, step, acc_in, acc_out, share, from_below, from_above, planes=None
):
    for k in range(POINTS[group]) if planes is None else planes:
        size = POINTS[group] * NP
        scale = get_layers(inv, 1, k * PLANE, size)
        for f in range(FIELDS):
            at = f * NODES + k * PLANE
            rate = summed(group, wr, f, k, size, from_below, from_above) * scale
            base = half[span(at, size), :]
            if acc_in is None or step == time_step:
                full = base + (base - state[span(at, size), :])
            if step == time_step:
                base = full
            v[span(at, size), :] = base + step * rate
            before = full if acc_in is None else acc_in[span(at, size), :]
            acc_out[span(at, size), :] = before + share * rate


def second_kernel(
    ids, block, recv, count, from_below, from_above, state, w, qw, flow_at, les_mat, ape_mat, place,
    place_edge, wr_in,
    v, inv_out, acc_out, half_out, acc_edges, up_out, down_out, g, vb, src, edge, flow, sems,
):
    cap, peers = recv.shape
    weights_at = span(FIELDS * PLANE, PLANE)

    def source():
        up = NA - 1
        masks = lane_masks()
        tiles = []
        for t in range(TILES):
            parts = [
                block[pl.ds(t * cap + c, peers, stride=TILES * cap), :] for c in range(cap)
            ]
            tiles.append(jnp.concatenate(parts, axis=0))
        tables_at = span((FIELDS + 1) * PLANE, cap)
        own = columns(targets(recv, count))
        below = columns(from_below[tables_at, 0:peers])
        above = columns(from_above[tables_at, 0:peers])
        own = pick_sum(
            jnp.concatenate(tiles[: TILES - 2], axis=1), own, cap, slice(0, 2 * LAYER)
        )
        lo_edge = pick_sum(tiles[TILES - 2], above, cap, slice(0, LAYER))
        hi_edge = pick_sum(tiles[TILES - 1], below, cap, slice(LAYER, 2 * LAYER))
        for m in range(3):
            high, low = split(own[m * COMP : (m + 1) * COMP])
            full = dot(place[...], jnp.concatenate([high, low], axis=0))
            size = NA * PLANE
            put_layers(src, 3, m * NODES, full * w[0:size, :])
            high, low = split(hi_edge[m * EDGE : (m + 1) * EDGE])
            full = dot(place_edge[...], jnp.concatenate([high, low], axis=0))
            edge[span(m * PLANE, PLANE), :] = full * from_below[weights_at, :]
            high, low = split(lo_edge[m * EDGE : (m + 1) * EDGE])
            full = dot(place_edge[...], jnp.concatenate([high, low], axis=0))
            edge[span((3 + m) * PLANE, PLANE), :] = full * from_above[weights_at, :]
        sum_in_plane(src, 6 * NP, up, masks)
        sum_in_plane(edge, 6, up, masks)
        sum_inner(src, 3, up)
        add_planes(src, up, edge.at[0 : 3 * PLANE], edge.at[3 * PLANE : 6 * PLANE], 3)
        size = NA * NP
        for k in range(NA):
            scale = (0.5 * time_step) * get_layers(inv_out, 1, k * PLANE, size)
            for f in range(FIELDS):
                at = f * NODES + k * PLANE
                value = state[span(at, size), :]
                if f < 3:
                    value = value + scale * get_layers(src, 3, at, size)
                half_out[span(at, size), :] = value

    def body(group):
        up = POINTS[group] - 1
        copies = flow_copies(flow_at, flow, up, sems) if group == 1 else []
        for copy in copies:
            copy.start()
        inv_out[...] = qw[...]
        edge[0:PLANE, :] = from_below[weights_at, :]
        edge[PLANE : 2 * PLANE, :] = from_above[weights_at, :]
        sum_in_plane(edge, 2, up, lane_masks())
        add_planes(inv_out, up, edge.at[0:PLANE], edge.at[PLANE : 2 * PLANE], 1)
        inv_out[...] = 1.0 / inv_out[...]
        if group == 1:
            source()
        else:
            half_out[...] = state[...]
        update(group, half_out, state, wr_in, inv_out, v, 0.5 * time_step, None, acc_out,
               time_step / 6.0, from_below, from_above)
        take_edges(group, v, vb)
        take_edges(group, acc_out, acc_edges)
        for copy in copies:
            copy.wait()
        edge_stage(group, (les_mat, ape_mat)[group], v, vb, w, flow, g, up_out, down_out)

    each_group(ids, body)


def edge_rate(group, f, from_below, from_above, down, up_planes, inv):
    size = POINTS[group] * NP
    at = span(f * PLANE, size)
    low = down[at, :] + from_below[at, :]
    high = up_planes[at, :] + from_above[at, :]
    low = low * inv[span(0, size), :]
    high = high * inv[span(NODES + (POINTS[group] - 1) * PLANE, size), :]
    return jnp.concatenate([low, high], axis=1)


def edge_step_kernel(
    step, ids, from_below, from_above, down, up_planes, v, half, state, w, inv, flow, les_mat,
    ape_mat, acc_in,
    vb, acc_edges, up_out, down_out, g,
):
    def body(group):
        up = POINTS[group] - 1
        size = POINTS[group] * NP
        for f in range(FIELDS):
            rate = edge_rate(group, f, from_below, from_above, down, up_planes, inv)
            base = edge_lanes(half, f * NODES, up, size)
            if step == time_step:
                base = base + (base - edge_lanes(state, f * NODES, up, size))
            put_edges(vb, f * PLANE, base + step * rate)
            before = get_edges(acc_in, f * PLANE, size)
            put_edges(acc_edges, f * PLANE, before + (time_step / 3.0) * rate)
        edge_stage(group, (les_mat, ape_mat)[group], v, vb, w, flow, g, up_out, down_out)

    each_group(ids, body)


def inner_kernel(step, ids, v_in, *refs):
    if step == 0.5 * time_step:
        half, state, w, inv, flow, les_mat, ape_mat, acc_in, v_out, acc_out, g, gz, wr = refs
        v = v_in
    else:
        vb, half, state, w, inv, flow, les_mat, ape_mat, acc_in = refs[:9]
        if step is None:
            acc_out, g, gz, wr, v, result, sems = refs[9:]
        else:
            v_out, acc_out, g, gz, wr, v = refs[9:]

    def body(group):
        if v is not v_in:
            v[...] = v_in[...]
            for f in range(FIELDS):
                size = POINTS[group] * NP
                up = POINTS[group] - 1
                value = get_edges(vb, f * PLANE, size)
                v[span(f * NODES, size), :LAYER] = value[:, :LAYER]
                v[span(f * NODES + up * PLANE, size), LAYER:] = value[:, LAYER:]
        copies = []

        def after(k):
            if step is None:
                finish(group, wr, inv, acc_in, result, k)
                send_out(k)
            else:
                update(group, half, state, wr, inv, v_out, step, acc_in, acc_out, time_step / 3.0,
                       None, None, (k,))

        def send_out(k):
            for f in range(FIELDS):
                at = span(f * NODES + k * PLANE, PLANE)
                copy = pltpu.make_async_copy(
                    result.at[at, :], acc_out.at[at, :], sems.at[k * FIELDS + f]
                )
                copy.start()
                copies.append(copy)

        if step is None:
            for k in range(POINTS[group], NP):
                finish(group, wr, inv, acc_in, result, k)
                send_out(k)
        inner_stage(group, (les_mat, ape_mat)[group], v, w, flow, g, gz, wr, after)
        for copy in copies:
            copy.wait()

    each_group(ids, body)


def finish(group, wr, inv, acc_in, out, k):
    points = POINTS[group]
    size = points * NP
    keep = lax.broadcasted_iota(jnp.int32, (size, 2 * LAYER), 0) % NP < points
    for f in range(FIELDS):
        at = f * NODES + k * PLANE
        done = 0
        if k < points:
            scale = get_layers(inv, 1, k * PLANE, size) * (time_step / 6.0)
            rate = summed(group, wr, f, k, size, None, None) * scale
            value = acc_in[span(at, size), :] + rate
            if points < NP:
                value = jnp.where(keep, value, 0.0)
            out[span(at, size), :] = value
            done = size
        if done < PLANE:
            out[span(at + done, PLANE - done), :] = jnp.zeros((PLANE - done, 2 * LAYER), f32)


def last_kernel(
    ids, from_below, from_above, down, up_planes, inv, acc_edges, inner, out, planes, sems
):
    def body(group):
        points = POINTS[group]
        size = points * NP
        keep = lax.broadcasted_iota(jnp.int32, (size, 2 * LAYER), 0) % NP < points
        copies = []
        for f in range(FIELDS):
            rate = edge_rate(group, f, from_below, from_above, down, up_planes, inv)
            value = get_edges(acc_edges, f * PLANE, size) + (time_step / 6.0) * rate
            if points < NP:
                value = jnp.where(keep, value, 0.0)
            put_edges(planes, f * PLANE, value)
            for side in range(2):
                row = f * NODES + side * (points - 1) * PLANE
                copies.append(
                    pltpu.make_async_copy(
                        planes.at[span((side * FIELDS + f) * PLANE, size), :],
                        out.at[span(row, size), side * LAYER : (side + 1) * LAYER],
                        sems.at[side * FIELDS + f],
                    )
                )
                copies[-1].start()
        for copy in copies:
            copy.wait()

    each_group(ids, body)


SMEM = pl.BlockSpec(memory_space=pltpu.SMEM)
VMEM = pl.BlockSpec(memory_space=pltpu.VMEM)


def call(kernel, args, outs, scratch, megabytes):
    return pl.pallas_call(
        kernel,
        out_shape=[jax.ShapeDtypeStruct(s, f32) for s in outs],
        in_specs=[SMEM] + [VMEM] * (len(args) - 1),
        out_specs=[VMEM] * len(outs),
        scratch_shapes=[pltpu.VMEM(s, f32) for s in scratch],
        compiler_params=pltpu.CompilerParams(vmem_limit_bytes=megabytes * 1024 * 1024),
    )(*args)


def on_device(state, mean_flow, jacobian, send_elem, recv_elem, recv_count):
    ids = lax.axis_index("grp").astype(jnp.int32).reshape(1)
    width = state.shape[-1]
    peers, cap = send_elem.shape[1:]
    state = state.reshape(FIELDS * NODES, width)
    flow = mean_flow.reshape(3 * NODES, width)
    jac = jacobian.reshape(NODES, width)
    send = jnp.swapaxes(send_elem, 1, 2).reshape(cap, peers)
    recv = jnp.swapaxes(recv_elem, 1, 2).reshape(cap, peers)
    les_mat, ape_mat = (jnp.asarray(m) for m in CONSTS["mats"])
    interp = jnp.asarray(CONSTS["interp"])
    place = jnp.asarray(CONSTS["place"])
    place_edge = jnp.asarray(CONSTS["place_edge"])
    full = (FIELDS * NODES, width)
    one = (NODES, width)
    layered = (2 * FIELDS * NODES, LAYER)
    one_layered = (2 * NODES, LAYER)
    thin = (FIELDS * PLANE, LAYER)
    edges = (2 * FIELDS * PLANE, LAYER)
    thick = ((FIELDS + 1) * PLANE + NP, LAYER)
    grads = (2, FIELDS, 2 * PLANE, width)
    size = lax.axis_size("elem")
    up_pairs = [(i, (i + 1) % size) for i in range(size)]
    down_pairs = [(j, i) for i, j in up_pairs]

    def exchange(up_planes, down_planes):
        return (
            lax.ppermute(up_planes, "elem", up_pairs),
            lax.ppermute(down_planes, "elem", down_pairs),
        )

    hbm = pl.BlockSpec(memory_space=pltpu.HBM)
    (block,) = pl.pallas_call(
        block_kernel,
        out_shape=[jax.ShapeDtypeStruct((TILES * cap * peers, LAYER), f32)],
        in_specs=[SMEM] + [hbm] * 4,
        out_specs=[VMEM],
        scratch_shapes=[
            pltpu.VMEM((3 * NODES, width), f32),
            pltpu.VMEM(les_mat.shape, bf16),
            pltpu.VMEM(interp.shape, bf16),
            pltpu.VMEM((cap, peers), jnp.int32),
            pltpu.VMEM(grads, f32),
            pltpu.VMEM((3 * NODES, width), f32),
            pltpu.VMEM((BLOCK, width), f32),
            pltpu.SemaphoreType.DMA((9,)),
        ],
        compiler_params=pltpu.CompilerParams(vmem_limit_bytes=62 * 1024 * 1024),
    )(ids, state, les_mat, interp, send)
    up_planes, down_planes = pl.pallas_call(
        edge_kernel,
        out_shape=[jax.ShapeDtypeStruct(thick, f32)] * 2,
        in_specs=[SMEM] + [VMEM] * 2 + [hbm] + [VMEM] * 4,
        out_specs=[VMEM] * 2,
        scratch_shapes=[
            pltpu.VMEM((3 * NODES, width), f32),
            pltpu.VMEM(grads[1:], f32),
            pltpu.VMEM(one, f32),
            pltpu.VMEM(edges, f32),
            pltpu.SemaphoreType.DMA((6,)),
        ],
        compiler_params=pltpu.CompilerParams(vmem_limit_bytes=8 * 1024 * 1024),
    )(ids, state, jac, flow, les_mat, ape_mat, recv, recv_count)
    from_below, from_above = exchange(up_planes, down_planes)
    block = lax.all_to_all(block, "elem", split_axis=0, concat_axis=0, tiled=True)
    block, from_below, from_above, late_ids = lax.optimization_barrier(
        (block, from_below, from_above, ids)
    )
    wr, w, qw = call(
        first_kernel,
        (late_ids, state, jac, flow, les_mat, ape_mat),
        [layered, one, one_layered],
        [grads, full],
        12,
    )
    block = lax.ppermute(block, "grp", [(0, 1)])
    v, inv, acc, half, acc_edges, up_planes, down_planes = pl.pallas_call(
        second_kernel,
        out_shape=[
            jax.ShapeDtypeStruct(s, f32)
            for s in (full, one_layered, full, full, edges, thin, thin)
        ],
        in_specs=[SMEM] + [VMEM] * 8 + [hbm] + [VMEM] * 5,
        out_specs=[VMEM] * 7,
        scratch_shapes=[
            pltpu.VMEM(s, f32)
            for s in (grads[1:], edges, (6 * NODES, LAYER), (6 * PLANE, LAYER), (3 * NODES, width))
        ]
        + [pltpu.SemaphoreType.DMA((6,))],
        compiler_params=pltpu.CompilerParams(vmem_limit_bytes=24 * 1024 * 1024),
    )(
        ids, block, recv, recv_count, from_below, from_above, state, w, qw, flow, les_mat,
        ape_mat, place, place_edge, wr,
    )
    vb = None
    for step in (0.5 * time_step, time_step, None):
        from_below, from_above = exchange(up_planes, down_planes)

        def inner(*refs, step=step):
            inner_kernel(step, *refs)

        def edge_step(*refs, step=step):
            edge_step_kernel(step, *refs)

        rest = (half, state, w, inv, flow, les_mat, ape_mat, acc)
        if vb is None:
            v, acc = call(inner, (ids, v) + rest, [full, full], [grads, full, layered], 24)
        elif step is not None:
            v, acc = call(inner, (ids, v, vb) + rest, [full, full], [grads, full, layered, full], 24)
        else:
            out = pl.pallas_call(
                inner,
                out_shape=jax.ShapeDtypeStruct(full, f32),
                in_specs=[SMEM] + [VMEM] * 10,
                out_specs=hbm,
                scratch_shapes=[pltpu.VMEM(s, f32) for s in (grads, full, layered, full, full)]
                + [pltpu.SemaphoreType.DMA((FIELDS * NP,))],
                compiler_params=pltpu.CompilerParams(vmem_limit_bytes=24 * 1024 * 1024),
            )(ids, v, vb, *rest)
            break
        vb, acc_edges, up_planes, down_planes = call(
            edge_step,
            (ids, from_below, from_above, down_planes, up_planes, v, half, state, w, inv, flow,
             les_mat, ape_mat, acc_edges),
            [edges, edges, thin, thin],
            [grads[1:]],
            14,
        )
    out = pl.pallas_call(
        last_kernel,
        out_shape=jax.ShapeDtypeStruct(full, f32),
        in_specs=[SMEM] + [VMEM] * 6 + [hbm],
        out_specs=hbm,
        scratch_shapes=[pltpu.VMEM(edges, f32), pltpu.SemaphoreType.DMA((2 * FIELDS,))],
        input_output_aliases={7: 0},
        compiler_params=pltpu.CompilerParams(vmem_limit_bytes=6 * 1024 * 1024),
    )(ids, from_below, from_above, down_planes, up_planes, inv, acc_edges, out)
    return out.reshape(1, FIELDS, NODES, width)


def solution(mesh):
    placed = (
        P("grp", None, None, "elem"),
        P(None, None, "elem"),
        P("grp", None, "elem"),
        P("elem", None, None),
        P("elem", None, None),
        P("elem", None),
    )
    return jax.shard_map(
        on_device,
        mesh=mesh,
        in_specs=placed,
        out_specs=P("grp", None, None, "elem"),
        check_vma=False,
    )
```
